256 devices in a mesh: curve: 64 (over z, y_lo, x), mp: 4 (over y_hi, core).
Axes of the slice: x: 4, y: 4 (y_hi: 2, y_lo: 2; y = y_hi * 2 + y_lo), z: 8, core: 2. Of those that a mesh axis runs over, the one named last changes fastest.
Arguments:
- points: bfloat16 [192, 1024, 512], P('curve'), may hold values from -6 to 6
- order: int32 [192, 1024], P('curve'), may hold values from 0 to 1023, each once within a row
- counts: int32 [64], P('curve'), may hold values from 1 to 3, as said below
- cotangent: bfloat16 [192, 1024, 512], P('curve'), may hold values from -6 to 6
- norm_gain: float32 [512], replicated, may hold values from 0.5 to 1.5
- w_qkv: bfloat16 [512, 3, 512], P(None, None, 'mp')
- w_out: bfloat16 [512, 512], P('mp'), may hold values from -0.25 to 0.25
Outputs:
- grad_points: bfloat16 [192, 1024, 512], P('curve', None, 'mp')
- grad_gain: float32 [512], P('mp')
- grad_qkv: float32 [512, 3, 512], P(None, None, 'mp')
- grad_out: float32 [512, 512], P('mp')
The draws below stay inside these ranges and needn't reach their ends.
Inputs may be any that keep to these rules, and one draw needn't show every extreme that they name: `counts`: in every aligned group of 4 indices of curve one index, at one of the group's first three places, holds 3; the index after it holds 1; every other index holds 1.
All inputs are finite; a program needn't handle non-finite values.
Results may differ from the reference program's by a relative error of at most 0.013.
Values may be sent and summed in bfloat16 or wider, within the bound.
No kernel may reach another device: no remote copies, remote signals or barrier semaphores. Data moves between devices by JAX's collectives and lax.ppermute only.
A program may use at most 128 MiB of HBM per device.

```python
import math
import jax
import jax.numpy as jnp
from jax import lax

D = 512
HEADS = 8
PATCH = 1024
CAP = 3
SLOTS = 192
N_CURVE = 64
N_MP = 4


def draw_counts(key, part):
    key = jax.random.fold_in(key, 5)
    first_key, second_key = jax.random.split(key)
    groups = N_CURVE // 4
    spots = jax.random.randint(first_key, (groups,), 0, 3)
    lights = jax.random.randint(second_key, (groups, 4), 1, CAP - 1)
    position = jnp.arange(4)[None, :]
    table = jnp.where(position == spots[:, None] + 1, 1, lights)
    table = jnp.where(position == spots[:, None], CAP, table)
    return table.reshape(N_CURVE).astype(jnp.int32)


def draw_w_qkv(key, part):
    key = jax.random.fold_in(key, 11)
    first_key = jax.random.fold_in(key, 0)
    return (jax.random.normal(first_key, (D, 3, D), jnp.float32) * D ** (-0.5)).astype(jnp.bfloat16)


def steps_of(rng, dims, cuts, least, largest):
    def one(dim, blocks):
        heights = jax.random.uniform(jax.random.fold_in(jax.random.fold_in(rng, 6), dim), (blocks,), jnp.float32, least / len(cuts), largest / len(cuts))
        return jnp.repeat(jnp.exp(heights), dims[dim] // blocks).reshape((-1,) + (1,) * (len(dims) - dim - 1))

    gain = one(*cuts[0])
    for cut in cuts[1:]:
        gain = gain * one(*cut)
    return gain


def noise(rng, dims, deviation, reach, pieces=(), kind=jnp.bfloat16):
    entries = jax.random.normal(rng, dims, jnp.float32) * deviation
    if len(pieces) > 0:
        entries = steps_of(rng, dims, pieces, -0.22, 0.18) * entries
    return jnp.clip(entries, min=-reach, max=reach).astype(kind)


def setup_inputs(seed: int = 0) -> dict:
    seeds = jax.random.split(jax.random.key(seed), 8)
    return {
        "points": noise(seeds[0], (SLOTS, PATCH, D), 1.0, 6.0, ((0, 64),)),
        "order": jax.vmap(lambda own: jax.random.permutation(own, PATCH))(jax.random.split(seeds[1], SLOTS)).reshape((SLOTS, PATCH)).astype(jnp.int32),
        "counts": draw_counts(jax.random.fold_in(seeds[7], 71), 0),
        "cotangent": noise(seeds[3], (SLOTS, PATCH, D), 1.0, 6.0, ((0, 64),)),
        "norm_gain": jnp.clip(1.0 + 0.1 * jax.random.normal(seeds[4], (D,), jnp.float32), 0.5, 1.5),
        "w_qkv": draw_w_qkv(jax.random.fold_in(seeds[7], 71), 0),
        "w_out": noise(seeds[6], (D, D), D ** -0.5, 0.25, ((0, 4),)),
    }


EPSILON = 1e-05

def norm_rows(rows, norm_gain):
    values = rows.astype(jnp.float32)
    centre = values - lax.optimization_barrier(jnp.mean(values, axis=-1, keepdims=True))
    inverse = lax.rsqrt(lax.optimization_barrier(jnp.mean(centre * centre, axis=-1, keepdims=True)) + EPSILON)
    unit = centre * inverse
    return (unit, inverse, (unit * norm_gain).astype(jnp.bfloat16))

def group_terms(normed, weight_qkv, weight_out, grad_rows):
    head_size = D // HEADS
    row_count = normed.shape[0]
    group_width = weight_out.shape[0]
    group_heads = group_width // head_size
    factor = head_size ** (-0.5)
    normed_f = normed.astype(jnp.float32)
    grad_f = grad_rows.astype(jnp.float32)
    projected = jnp.einsum('kd,dtg->tkg', normed_f, weight_qkv.astype(jnp.float32)).astype(jnp.bfloat16)
    queries = projected[0].reshape(row_count, group_heads, head_size).astype(jnp.float32)
    key_rows = projected[1].reshape(row_count, group_heads, head_size).astype(jnp.float32)
    value_rows = projected[2].reshape(row_count, group_heads, head_size).astype(jnp.float32)
    scores = jnp.einsum('qhe,khe->hqk', queries, key_rows) * factor
    highest = lax.optimization_barrier(jnp.max(scores, axis=-1, keepdims=True))
    expos = jnp.exp(scores - highest)
    probs = expos / lax.optimization_barrier(jnp.sum(expos, axis=-1, keepdims=True))
    probs_low = probs.astype(jnp.bfloat16).astype(jnp.float32)
    attended = jnp.einsum('hqk,khe->qhe', probs_low, value_rows).astype(jnp.bfloat16).reshape(row_count, group_width)
    grad_attended = jnp.einsum('kd,gd->kg', grad_f, weight_out.astype(jnp.float32)).astype(jnp.bfloat16)
    out_term = jnp.einsum('kg,kd->gd', attended.astype(jnp.float32), grad_f)
    grad_heads = grad_attended.reshape(row_count, group_heads, head_size).astype(jnp.float32)
    grad_values = jnp.einsum('hqk,qhe->khe', probs_low, grad_heads).astype(jnp.bfloat16)
    grad_probs = jnp.einsum('qhe,khe->hqk', grad_heads, value_rows)
    inner_sum = lax.optimization_barrier(jnp.sum(probs * grad_probs, axis=-1, keepdims=True))
    grad_scores = (probs * (grad_probs - inner_sum) * factor).astype(jnp.bfloat16).astype(jnp.float32)
    grad_queries = jnp.einsum('hqk,khe->qhe', grad_scores, key_rows).astype(jnp.bfloat16)
    grad_keys = jnp.einsum('hqk,qhe->khe', grad_scores, queries).astype(jnp.bfloat16)
    grad_projected = jnp.stack([grad_queries, grad_keys, grad_values]).reshape(3, row_count, group_width).astype(jnp.float32)
    qkv_term = jnp.einsum('kd,tkg->dtg', normed_f, grad_projected)
    group_normed = jnp.einsum('tkg,dtg->kd', grad_projected, weight_qkv.astype(jnp.float32)).astype(jnp.bfloat16)
    return (group_normed, qkv_term, out_term)

def patch_terms(patch_x, patch_dy, norm_gain, w_qkv, w_out):
    unit, inverse, normed = norm_rows(patch_x, norm_gain)
    group_width = D // N_MP
    grad_normed = jnp.zeros((PATCH, D), jnp.float32)
    qkv_terms = []
    out_terms = []
    for group in range(N_MP):
        low = group * group_width
        part_normed, qkv_term, out_term = group_terms(normed, w_qkv[:, :, low:low + group_width], w_out[low:low + group_width], patch_dy)
        grad_normed = grad_normed + part_normed.astype(jnp.float32)
        qkv_terms.append(qkv_term)
        out_terms.append(out_term)
    scaled = grad_normed * norm_gain
    branch = inverse * (scaled - lax.optimization_barrier(jnp.mean(scaled, axis=-1, keepdims=True)) - unit * lax.optimization_barrier(jnp.mean(scaled * unit, axis=-1, keepdims=True)))
    gain_term = lax.optimization_barrier(jnp.sum(grad_normed * unit, axis=0))
    return (branch, jnp.concatenate(qkv_terms, axis=2), jnp.concatenate(out_terms, axis=0), gain_term)

def reference(points, order, counts, cotangent, norm_gain, w_qkv, w_out):
    half_rows = PATCH // 2
    slot_rows = jnp.arange(SLOTS, dtype=jnp.int32)[:, None]
    series_x = points[slot_rows, order].reshape(N_CURVE, CAP, PATCH, D)
    series_dy = cotangent[slot_rows, order].reshape(N_CURVE, CAP, PATCH, D)
    places = jnp.arange(CAP, dtype=jnp.int32)[None, :]
    live = places < counts[:, None]
    onward = places + 1 < counts[:, None]

    def shifted(series):
        ahead = jnp.concatenate([series[:, 1:, :half_rows], series[:, :1, :half_rows]], axis=1)
        borrowed = jnp.roll(series[:, 0, :half_rows], -1, axis=0)[:, None]
        head_rows = jnp.where(onward[:, :, None, None], ahead, borrowed)
        return jnp.concatenate([series[:, :, half_rows:], head_rows], axis=2).reshape(SLOTS, PATCH, D)
    patch_x = shifted(series_x)
    patch_dy = shifted(series_dy)

    def compute(rows_x, rows_dy):
        return patch_terms(rows_x, rows_dy, norm_gain, w_qkv, w_out)

    def nothing(rows_x, rows_dy):
        return (jnp.zeros((PATCH, D), jnp.float32), jnp.zeros((D, 3, D), jnp.float32), jnp.zeros((D, D), jnp.float32), jnp.zeros((D,), jnp.float32))

    def visit(totals, item):
        rows_x, rows_dy, alive = item
        branch, qkv_term, out_term, gain_term = lax.cond(alive, compute, nothing, rows_x, rows_dy)
        return ((totals[0] + qkv_term, totals[1] + out_term, totals[2] + gain_term), branch)
    start = (jnp.zeros((D, 3, D), jnp.float32), jnp.zeros((D, D), jnp.float32), jnp.zeros((D,), jnp.float32))
    totals, branches = lax.scan(visit, start, (patch_x, patch_dy, live.reshape(SLOTS)))
    branches = branches.reshape(N_CURVE, CAP, PATCH, D)
    tail_part = branches[:, :, :half_rows]
    head_part = branches[:, :, half_rows:]
    into_next = jnp.where(onward[:, :, None, None], head_part, 0.0)
    front = jnp.concatenate([jnp.zeros_like(into_next[:, :1]), into_next[:, :-1]], axis=1)
    outer = lax.optimization_barrier(jnp.sum(jnp.where((live & jnp.logical_not(onward))[:, :, None, None], head_part, 0.0), axis=1))
    front = front.at[:, 0].add(jnp.roll(outer, 1, axis=0))
    placed = jnp.concatenate([front, tail_part], axis=2)
    grad_series = (series_dy.astype(jnp.float32) + placed).reshape(SLOTS, PATCH, D)
    grad_points = jnp.zeros((SLOTS, PATCH, D), jnp.float32).at[slot_rows, order].set(grad_series).astype(jnp.bfloat16)
    factor = 1.0 / math.sqrt(SLOTS * PATCH)
    return (grad_points, totals[2] * factor, totals[0] * factor, totals[1] * factor)
```

```python
import functools
import math

import jax
import jax.numpy as jnp
from jax import lax
from jax.experimental import pallas as pl
from jax.experimental.pallas import tpu as pltpu
from jax.sharding import PartitionSpec as P

D = 512
HEADS = 8
HEAD = D // HEADS
EPSILON = 1e-05
LOG2E = math.log2(math.e)

F32 = jnp.float32
BF16 = jnp.bfloat16
NT = (((1,), (1,)), ((), ()))
VMEM = pl.BlockSpec(memory_space=pltpu.VMEM)
SMEM = pl.BlockSpec(memory_space=pltpu.SMEM)


def mm(a, b):
    return jnp.dot(a, b, preferred_element_type=F32)


def mm_nt(a, b):
    return lax.dot_general(a, b, NT, preferred_element_type=F32)


def params(mib):
    return pltpu.CompilerParams(vmem_limit_bytes=mib * 1024 * 1024)


def cost(flops, bytes_accessed):
    return pl.CostEstimate(flops=flops, bytes_accessed=bytes_accessed, transcendentals=0)


def one_hot_rows(places, patch):
    count = places.shape[1]
    column = jnp.broadcast_to(places, (128, count)).T
    lanes = lax.broadcasted_iota(jnp.int32, (count, 128), 1)
    return jnp.concatenate(
        [(column == lanes + 128 * b).astype(BF16) for b in range(patch // 128)], axis=1
    )


def halo_kernel(scal, order, points, cotangent, out):
    rows = out.shape[1]
    start = pl.multiple_of(scal[0] * rows, rows)
    chosen = one_hot_rows(order[0:1, pl.ds(start, rows)], points.shape[1])
    out[0] = mm(chosen, points[0]).astype(BF16)
    out[1] = mm(chosen, cotangent[0]).astype(BF16)


def norm_half(x, gain, own):
    values = x.astype(F32)
    mean = jnp.mean(values, axis=1, keepdims=True)
    centre = values - mean
    inverse = lax.rsqrt(jnp.mean(centre * centre, axis=1, keepdims=True) + EPSILON)
    normed = (centre * inverse * gain).astype(BF16)
    unit = ((own.astype(F32) - mean) * inverse).T
    inverse_row = jnp.broadcast_to(inverse, (x.shape[0], 128)).T[0:8]
    return normed, unit, inverse_row


def patch_core(nrm, dy, w3, wt, wo, prj, kr, vr, dat, acc, gp, att, wacc):
    rows = nrm.shape[0]
    block = 256
    prj[...] = mm_nt(wt[...], nrm[...]).astype(BF16)
    kr[...] = mm(nrm[...], w3[1]).astype(BF16)
    vr[...] = mm(nrm[...], w3[2]).astype(BF16)
    dat[...] = mm_nt(wo[...], dy[...]).astype(BF16)
    acc[...] = jnp.zeros_like(acc)
    scale = HEAD ** (-0.5) * LOG2E
    zeros = jnp.zeros((HEAD, block), BF16)

    def pad(x, h):
        return jnp.concatenate([x, zeros] if h == 0 else [zeros, x], axis=0)

    def step(i, carry):
        cols = pl.ds(pl.multiple_of(i * block, block), block)
        for h in range(2):
            lo = h * HEAD
            q = prj[lo:lo + HEAD, cols]
            scores = mm(kr[...], pad(q, h))
            high = jnp.max(scores, axis=0, keepdims=True) * scale
            expos = jnp.exp2(scores * scale - high)
            recip = 1.0 / jnp.sum(expos, axis=0, keepdims=True)
            low = expos.astype(BF16)
            attended = mm(prj[256 + lo:256 + lo + HEAD, :], low) * recip
            att[lo:lo + HEAD, cols] = attended.astype(BF16)
            grad = dat[lo:lo + HEAD, cols].astype(F32) * recip
            inner = jnp.sum(grad * attended, axis=0, keepdims=True)
            grad = grad.astype(BF16)
            grad_probs = mm(vr[...], pad(grad, h))
            grad_scores = (expos * (grad_probs - inner)).astype(BF16)
            dq = mm(prj[128 + lo:128 + lo + HEAD, :], grad_scores) * (HEAD ** (-0.5))
            gp[lo:lo + HEAD, cols] = dq.astype(BF16)
            acc[lo:lo + HEAD, :] += mm_nt(q, grad_scores)
            acc[128 + lo:128 + lo + HEAD, :] += mm_nt(grad, low)
        return carry

    lax.fori_loop(0, rows // block, step, 0)
    gp[128:256, :] = (acc[0:128] * (HEAD ** (-0.5))).astype(BF16)
    gp[256:384, :] = acc[128:256].astype(BF16)
    wacc[0:384] += mm(gp[...], nrm[...])
    wacc[384:512] += mm(att[...], dy[...])


def second_stat(gp, prj):
    return jnp.sum(gp[...].astype(F32) * prj[...].astype(F32), axis=0, keepdims=True)


def local_kernel(scal, order, points, cotangent, gain, w3, wo,
                 gp_i, unit_i, stat_i, wacc, nrm_l, dy_l, unit_l, stat_l, wt,
                 nrm, dy, own, prj, kr, vr, dat, acc, att):
    count = scal[2]
    patch = points.shape[1]
    half = patch // 2
    first = pl.multiple_of(scal[1] * 128, 128)
    for t in range(3):
        wt[128 * t:128 * t + 128, :] = w3[t].astype(F32).T.astype(BF16)
    wacc[...] = jnp.zeros_like(wacc)

    def gather(slot, side, into_x, into_dy, at):
        chosen = one_hot_rows(order[pl.ds(slot, 1), half * side:half * side + half], patch)
        x = mm(chosen, points[slot]).astype(BF16)
        into_dy[at:at + half, :] = mm(chosen, cotangent[slot]).astype(BF16)
        own[...] = x
        normed, unit, inverse = norm_half(x, gain[...], own[:, pl.ds(first, 128)])
        into_x[at:at + half, :] = normed
        return unit, inverse

    def interior(p, carry):
        for side in range(2):
            unit, inverse = gather(p + side, 1 - side, nrm, dy, half * side)
            unit_i[p, :, half * side:half * side + half] = unit
            stat_i[p, :, half * side:half * side + half] = inverse
        gp_p = gp_i.at[p]
        patch_core(nrm, dy, w3, wt, wo, prj, kr, vr, dat, acc, gp_p, att, wacc)
        stat_i[p, 1:2, :] = second_stat(gp_p, prj)
        return carry

    lax.fori_loop(0, count - 1, interior, 0)
    unit, inverse = gather(count - 1, 1, nrm_l, dy_l, 0)
    unit_l[...] = unit
    stat_l[...] = inverse


def last_kernel(factor, scal, mine, other, nrm_l, dy_l, unit_l, stat_l, wacc_i, gain, w3, wt, wo,
                gp, unit_o, stat_o, pieces, gain_o,
                nrm, dy, own, prj, kr, vr, dat, acc, att, wacc):
    half = nrm_l.shape[0]
    part = half // 2
    first = pl.multiple_of(scal[1] * 128, 128)
    is_first = scal[0] == 0
    nrm[0:half, :] = nrm_l[...]
    dy[0:half, :] = dy_l[...]
    unit_o[:, 0:half] = unit_l[...]
    stat_o[:, 0:half] = stat_l[...]
    own_at = pl.multiple_of(scal[0] * part, part)
    other_at = pl.multiple_of((1 - scal[0]) * part, part)
    own[pl.ds(own_at, part), :] = mine[0]
    own[pl.ds(other_at, part), :] = other[0]
    dy[pl.ds(half + own_at, part), :] = mine[1]
    dy[pl.ds(half + other_at, part), :] = other[1]
    normed, unit, inverse = norm_half(own[...], gain[...], own[:, pl.ds(first, 128)])
    nrm[half:, :] = normed
    unit_o[:, half:] = unit
    stat_o[:, half:] = inverse
    wacc[...] = wacc_i[...]
    patch_core(nrm, dy, w3, wt, wo, prj, kr, vr, dat, acc, gp, att, wacc)
    stat_o[1:2, :] = second_stat(gp, prj)
    total = wacc[0:384] * factor
    gain_row = jnp.sum(total * wt[...].astype(F32), axis=0, keepdims=True) / gain[...]
    gain_o[...] = jnp.broadcast_to(gain_row, gain_o.shape)
    for r in range(16):
        for c in range(4):
            block = wacc[32 * r:32 * r + 32, 128 * c:128 * c + 128]
            pieces[4 * r + c] = (block * factor).astype(BF16)


def spread_kernel(scal, gp_i, gp_l, stat_i, stat_l, gain_row, w3, gain_column,
                  send, keep, stats, grads):
    core, count = scal[0], scal[2]
    patch = gp_l.shape[1]
    weights = jnp.concatenate([w3[0], w3[1], w3[2]], axis=1)
    stats[:, 3 * patch:] = gain_row[...]

    def one(p, gp, stat):
        cols = pl.ds(pl.multiple_of(p * patch, patch), patch)
        grads[...] = mm(weights, gp).astype(BF16)
        mean = jnp.sum(grads[...].astype(F32) * gain_column[...], axis=0, keepdims=True)
        stats[0:1, cols] = mean
        stats[1:2, cols] = stat
        for j in range(2):
            kept = pl.multiple_of((2 * j + core) * 128, 128)
            sent = pl.multiple_of((2 * j + 1 - core) * 128, 128)
            keep[j, :, cols] = grads[pl.ds(kept, 128), :]
            send[j, :, cols] = grads[pl.ds(sent, 128), :]

    def interior(p, carry):
        one(p, gp_i[p], stat_i[p, 1:2, :])
        return carry

    lax.fori_loop(0, count - 1, interior, 0)
    one(2, gp_l[...], stat_l[1:2, :])


def pair_kernel(scal, keep, received, stats, stats_received, send, kept, stats_o):
    far = scal[3]
    send[...] = (keep[1 - far].astype(F32) + received[1 - far].astype(F32)).astype(BF16)
    kept[...] = keep[far].astype(F32) + received[far].astype(F32)
    stats_o[...] = stats[...] + stats_received[...]


def branch_kernel(scal, kept, received, stats, stats_received, unit_i, unit_l, stat_i, stat_l,
                  gain_column, branch, back, gain_o):
    count = scal[2]
    patch = unit_l.shape[1]
    first = pl.multiple_of(scal[1] * 128, 128)
    own_gain = gain_column[pl.ds(first, 128), :]

    def one(p, unit, inverse):
        cols = pl.ds(pl.multiple_of(p * patch, patch), patch)
        scaled = (kept[:, cols] + received[:, cols].astype(F32)) * own_gain
        mean = (stats[0:1, cols] + stats_received[0:1, cols]) * (1.0 / D)
        slope = (stats[1:2, cols] + stats_received[1:2, cols]) * (1.0 / D)
        return (inverse * (scaled - mean - unit * slope)).astype(BF16)

    def interior(p, carry):
        branch[p] = one(p, unit_i[p], stat_i[p, 0:1, :])
        return carry

    lax.fori_loop(0, count - 1, interior, 0)
    last = one(2, unit_l[...], stat_l[0:1, :])
    branch[2] = last
    back[...] = last[:, patch // 2:]
    at = pl.ds(pl.multiple_of(3 * patch + first, 128), 128)
    gain_o[...] = stats[:, at] + stats_received[:, at]


def total_kernel(received, gain, out):
    def add(i, total):
        return total + received[i].astype(F32)

    total = lax.fori_loop(0, received.shape[0], add, jnp.zeros(received.shape[1:], F32), unroll=8)
    low = total.astype(BF16)
    gain_low = gain[...].astype(BF16)

    def put(i, carry):
        out[i, 0:32, :] = low
        out[i, 32:40, :] = gain_low
        return carry

    lax.fori_loop(0, received.shape[0], put, 0, unroll=8)


def place_kernel(scal, order, cotangent, branch, returned, out, placed):
    slot = pl.program_id(0)
    count = scal[2]
    patch = out.shape[1]
    half = patch // 2

    @pl.when(slot >= count)
    def _():
        out[...] = cotangent[...]

    @pl.when(slot < count)
    def _():
        @pl.when(slot == 0)
        def _():
            placed[:, 0:half] = returned[...]

        @pl.when(slot > 0)
        def _():
            placed[:, 0:half] = branch[jnp.maximum(slot - 1, 0), :, half:]

        placed[:, half:] = branch[jnp.where(slot + 1 < count, slot, 2), :, 0:half]
        places = order[pl.ds(slot, 1), :]
        rows = 256
        for r in range(patch // rows):
            index = lax.broadcasted_iota(jnp.int32, (rows, patch), 0) + rows * r
            chosen = (index == places).astype(BF16)
            moved = mm_nt(chosen, placed[...])
            own = cotangent[0, rows * r:rows * r + rows, :].astype(F32)
            out[0, rows * r:rows * r + rows, :] = (own + moved).astype(BF16)


def finish_kernel(received, qkv, out, gain):
    gain[...] = jnp.sum(received[:, 32:40, :].astype(F32), axis=0)
    for t in range(3):
        for c in range(4):
            block = jnp.concatenate(
                [received[4 * (4 * t + r) + c, 0:32, :].astype(F32) for r in range(4)], axis=0
            )
            qkv[t, 128 * c:128 * c + 128, :] = block.T
    for r in range(4):
        for c in range(4):
            out[32 * r:32 * r + 32, 128 * c:128 * c + 128] = received[
                4 * (12 + r) + c, 0:32, :
            ].astype(F32)


def shards(points, order, counts, cotangent, norm_gain, w_qkv, w_out):
    slots, patch, width = points.shape
    half = patch // 2
    curve = lax.axis_size("curve")
    model_part = lax.axis_index("mp")
    core = model_part % 2
    far = model_part // 2
    scal = jnp.stack([core, model_part, counts[0], far]).astype(jnp.int32)
    gain_row = norm_gain.reshape(1, width)
    gain_column = norm_gain.reshape(width, 1)
    w3 = jnp.transpose(w_qkv, (1, 0, 2))
    sds = jax.ShapeDtypeStruct

    def passed(x, by):
        return lax.ppermute(x, "curve", [(i, (i + by) % curve) for i in range(curve)])

    def swapped(x, bit):
        return lax.ppermute(x, "mp", [(i, i ^ bit) for i in range(4)])

    slot_block = pl.BlockSpec((1, patch, width), lambda i: (0, 0, 0))
    head = pl.pallas_call(
        halo_kernel,
        grid=(1,),
        in_specs=[SMEM, pl.BlockSpec((slots, patch), lambda i: (0, 0)), slot_block, slot_block],
        out_specs=pl.BlockSpec((2, half // 2, width), lambda i: (0, 0, 0)),
        out_shape=sds((2, half // 2, width), BF16),
        compiler_params=params(32),
        name="halo",
    )(scal, order, points, cotangent)
    mine = passed(head, -1)

    work = [
        pltpu.VMEM((patch, width), BF16),
        pltpu.VMEM((patch, width), BF16),
        pltpu.VMEM((half, width), BF16),
        pltpu.VMEM((384, patch), BF16),
        pltpu.VMEM((patch, 128), BF16),
        pltpu.VMEM((patch, 128), BF16),
        pltpu.VMEM((128, patch), BF16),
        pltpu.VMEM((256, patch), F32),
        pltpu.VMEM((128, patch), BF16),
    ]
    gp_i, unit_i, stat_i, wacc, nrm_l, dy_l, unit_l, stat_l, wt = pl.pallas_call(
        local_kernel,
        in_specs=[SMEM] + [VMEM] * 6,
        out_specs=[VMEM] * 9,
        out_shape=[
            sds((slots - 1, 384, patch), BF16),
            sds((slots - 1, 128, patch), F32),
            sds((slots - 1, 8, patch), F32),
            sds((512, width), F32),
            sds((half, width), BF16),
            sds((half, width), BF16),
            sds((128, half), F32),
            sds((8, half), F32),
            sds((384, width), BF16),
        ],
        scratch_shapes=work,
        compiler_params=params(56),
        cost_estimate=cost(8 * 10**9, 16 * 10**6),
        name="local",
    )(scal, order, points, cotangent, gain_row, w3, w_out)

    other = swapped(mine, 1)
    factor = 1.0 / math.sqrt(curve * slots * patch)
    gp_l, unit_l, stat_l, pieces, gain_part = pl.pallas_call(
        functools.partial(last_kernel, factor),
        in_specs=[SMEM] + [VMEM] * 11,
        out_specs=[VMEM] * 5,
        out_shape=[
            sds((384, patch), BF16),
            sds((128, patch), F32),
            sds((8, patch), F32),
            sds((64, 32, 128), BF16),
            sds((8, width), F32),
        ],
        scratch_shapes=work + [pltpu.VMEM((512, width), F32)],
        compiler_params=params(56),
        cost_estimate=cost(4 * 10**9, 8 * 10**6),
        name="last",
    )(scal, mine, other, nrm_l, dy_l, unit_l, stat_l, wacc, gain_row, w3, wt, w_out)

    received = lax.all_to_all(pieces, "curve", 0, 0)

    lanes = slots * patch
    send, keep, stats = pl.pallas_call(
        spread_kernel,
        in_specs=[SMEM] + [VMEM] * 7,
        out_specs=[VMEM] * 3,
        out_shape=[
            sds((2, 128, lanes), BF16),
            sds((2, 128, lanes), BF16),
            sds((8, lanes + width), F32),
        ],
        scratch_shapes=[pltpu.VMEM((width, patch), BF16)],
        compiler_params=params(48),
        cost_estimate=cost(2 * 10**9, 8 * 10**6),
        name="spread",
    )(scal, gp_i, gp_l, stat_i, stat_l, gain_part, w3, gain_column)
    near, near_stats = swapped(send, 1), swapped(stats, 1)
    send, kept, stats = pl.pallas_call(
        pair_kernel,
        in_specs=[SMEM] + [VMEM] * 4,
        out_specs=[VMEM] * 3,
        out_shape=[sds((128, lanes), BF16), sds((128, lanes), F32), sds((8, lanes + width), F32)],
        compiler_params=params(48),
        name="pair",
    )(scal, keep, near, stats, near_stats)
    away, away_stats = swapped(send, 2), swapped(stats, 2)
    branch, back, gain_own = pl.pallas_call(
        branch_kernel,
        in_specs=[SMEM] + [VMEM] * 9,
        out_specs=[VMEM] * 3,
        out_shape=[sds((slots, 128, patch), BF16), sds((128, half), BF16), sds((8, 128), F32)],
        compiler_params=params(48),
        name="branch",
    )(scal, kept, away, stats, away_stats, unit_i, unit_l, stat_i, stat_l, gain_column)
    returned = passed(back, 1)

    totals = pl.pallas_call(
        total_kernel,
        in_specs=[VMEM] * 2,
        out_specs=VMEM,
        out_shape=sds((64, 40, 128), BF16),
        compiler_params=params(32),
        name="total",
    )(received, gain_own)
    gathered = lax.all_to_all(totals, "curve", 0, 0)

    grad_points = pl.pallas_call(
        place_kernel,
        grid_spec=pltpu.PrefetchScalarGridSpec(
            num_scalar_prefetch=1,
            grid=(slots,),
            in_specs=[
                pl.BlockSpec((slots, patch), lambda i, s: (0, 0)),
                pl.BlockSpec((1, patch, 128), lambda i, s: (i, 0, s[1])),
                pl.BlockSpec((slots, 128, patch), lambda i, s: (0, 0, 0)),
                pl.BlockSpec((128, half), lambda i, s: (0, 0)),
            ],
            out_specs=pl.BlockSpec((1, patch, 128), lambda i, s: (i, 0, 0)),
            scratch_shapes=[pltpu.VMEM((128, patch), BF16)],
        ),
        out_shape=sds((slots, patch, 128), BF16),
        compiler_params=params(32),
        name="place",
    )(scal, order, cotangent, branch, returned)

    grad_qkv, grad_out, grad_gain = pl.pallas_call(
        finish_kernel,
        in_specs=[VMEM],
        out_specs=[VMEM] * 3,
        out_shape=[sds((3, width, 128), F32), sds((128, width), F32), sds((8, 128), F32)],
        compiler_params=params(32),
        name="finish",
    )(gathered)
    return grad_points, grad_gain[0], jnp.transpose(grad_qkv, (1, 0, 2)), grad_out


def solution(mesh):
    in_specs = (
        P("curve", None, None),
        P("curve", None),
        P("curve"),
        P("curve", None, None),
        P(),
        P(None, None, "mp"),
        P("mp", None),
    )
    out_specs = (P("curve", None, "mp"), P("mp"), P(None, None, "mp"), P("mp", None))
    return jax.shard_map(shards, mesh=mesh, in_specs=in_specs, out_specs=out_specs, check_vma=False)
```

```python
import functools
import math

import jax
import jax.numpy as jnp
from jax import lax
from jax.experimental import pallas as pl
from jax.experimental.pallas import tpu as pltpu
from jax.sharding import PartitionSpec as P

D = 512
HEADS = 8
HEAD = D // HEADS
EPSILON = 1e-05
SCALE = HEAD ** (-0.5) * math.log2(math.e)

F32 = jnp.float32
BF16 = jnp.bfloat16
NT = (((1,), (1,)), ((), ()))
VMEM = pl.BlockSpec(memory_space=pltpu.VMEM)
SMEM = pl.BlockSpec(memory_space=pltpu.SMEM)
ANY = pl.BlockSpec(memory_space=pl.ANY)


def mm(a, b):
    return jnp.dot(a, b, preferred_element_type=F32)


def mm_nt(a, b):
    return lax.dot_general(a, b, NT, preferred_element_type=F32)


def params(mib):
    return pltpu.CompilerParams(vmem_limit_bytes=mib * 1024 * 1024)


def cost(flops, bytes_accessed):
    return pl.CostEstimate(flops=flops, bytes_accessed=bytes_accessed, transcendentals=0)


def one_hot_rows(places, patch):
    count = places.shape[1]
    column = jnp.broadcast_to(places, (128, count)).T
    lanes = lax.broadcasted_iota(jnp.int32, (count, 128), 1)
    return jnp.concatenate(
        [(column == lanes + 128 * b).astype(BF16) for b in range(patch // 128)], axis=1
    )


def halo_kernel(scal, order, first_x, first_dy, last_x, last_dy, pull, push, chosen):
    rows = pull.shape[1]
    patch = first_x.shape[1]

    @pl.when(pl.program_id(0) == 0)
    def _():
        for k, slot, base in ((0, 0, 0), (1, order.shape[0] - 1, patch // 2)):
            at = pl.ds(pl.multiple_of(base + scal[0] * rows, rows), rows)
            chosen[k] = one_hot_rows(order[slot:slot + 1, at], patch)

    pull[0] = mm(chosen[0], first_x[0]).astype(BF16)
    pull[1] = mm(chosen[0], first_dy[0]).astype(BF16)
    push[0] = mm(chosen[1], last_x[0]).astype(BF16)
    push[1] = mm(chosen[1], last_dy[0]).astype(BF16)


def norm_half(x, gain, own):
    values = x.astype(F32)
    mean = jnp.mean(values, axis=1, keepdims=True)
    centre = values - mean
    inverse = lax.rsqrt(jnp.mean(centre * centre, axis=1, keepdims=True) + EPSILON)
    normed = (centre * inverse * gain).astype(BF16)
    unit = ((own.astype(F32) - mean) * inverse).T.astype(BF16)
    inverse_row = jnp.broadcast_to(inverse, (x.shape[0], 128)).T[0:8]
    return normed, unit, inverse_row


def project(nrm, dy, w3, wt, wo, prj, kr, vr, dat):
    prj[0:128, :] = (mm_nt(wt[0:128, :], nrm[...]) * SCALE).astype(BF16)
    prj[128:384, :] = mm_nt(wt[128:384, :], nrm[...]).astype(BF16)
    kr[...] = mm(nrm[...], w3[1]).astype(BF16)
    vr[...] = mm(nrm[...], w3[2]).astype(BF16)
    dat[...] = mm_nt(wo[...], dy[...]).astype(BF16)


def attend(prj, kr, vr, dat, gp, att):
    zeros = jnp.zeros((HEAD, prj.shape[1]), BF16)

    def pad(x, h):
        return jnp.concatenate([x, zeros] if h == 0 else [zeros, x], axis=0)

    def soft(scores):
        expos = jnp.exp2(scores - jnp.max(scores, axis=0, keepdims=True))
        recip = 1.0 / jnp.sum(expos, axis=0, keepdims=True)
        return expos, expos.astype(BF16), recip

    def middle(lo, expos, low, recip):
        attended = mm(prj[256 + lo:256 + lo + HEAD, :], low) * recip
        att[lo:lo + HEAD, :] = attended.astype(BF16)
        grad = dat[lo:lo + HEAD, :].astype(F32) * recip
        inner = jnp.sum(grad * attended, axis=0, keepdims=True)
        grad = grad.astype(BF16)
        grad_probs = mm(vr[...], pad(grad, lo // HEAD))
        return grad, (expos * (grad_probs - inner)).astype(BF16)

    def end(lo, low, grad, grad_scores):
        dq = mm(prj[128 + lo:128 + lo + HEAD, :], grad_scores) * (HEAD ** (-0.5))
        gp[lo:lo + HEAD, :] = dq.astype(BF16)
        dk = mm_nt(prj[lo:lo + HEAD, :], grad_scores) * (HEAD ** (-0.5) / SCALE)
        gp[128 + lo:128 + lo + HEAD, :] = dk.astype(BF16)
        gp[256 + lo:256 + lo + HEAD, :] = mm_nt(grad, low).astype(BF16)

    heads = (0, HEAD)
    scores = [mm(kr[...], pad(prj[lo:lo + HEAD, :], lo // HEAD)) for lo in heads]
    softs = [soft(x) for x in scores]
    middles = [middle(lo, *x) for lo, x in zip(heads, softs)]
    for lo, x, y in zip(heads, softs, middles):
        end(lo, x[1], *y)


def patch_core(core, p, nrm, dy, w3, wt, wo, gain_column, send, keep, stats,
               prj, kr, vr, dat, att, wacc, gp, grads, done):
    project(nrm, dy, w3, wt, wo, prj, kr, vr, dat)
    attend(prj, kr, vr, dat, gp, att)
    patch = gp.shape[1]
    cols = pl.ds(pl.multiple_of(p * patch, patch), patch)
    weights = jnp.concatenate([w3[0], w3[1], w3[2]], axis=1)
    grads[...] = mm(weights, gp[...]).astype(BF16)
    copies = []
    for j in range(2):
        for k, (block, into) in enumerate(((2 * j + 1 - core, send), (2 * j + core, keep))):
            rows = pl.ds(pl.multiple_of(block * 128, 128), 128)
            copies.append(
                pltpu.make_async_copy(grads.at[rows], into.at[j, :, cols], done.at[2 * j + k])
            )
            copies[-1].start()
    wacc[0:384] += mm(gp[...], nrm[...])
    wacc[384:512] += mm(att[...], dy[...])
    stats[0:1, cols] = jnp.sum(grads[...].astype(F32) * gain_column[...], axis=0, keepdims=True)
    stats[1:2, cols] = second_stat(gp, prj)
    for copy in copies:
        copy.wait()


def second_stat(gp, prj):
    product = gp[...].astype(F32) * prj[...].astype(F32)
    queries = jnp.sum(product[0:128], axis=0, keepdims=True) * (1.0 / SCALE)
    return queries + jnp.sum(product[128:384], axis=0, keepdims=True)


def gather_rows(scal, order, points, cotangent, gain, own, slot, side, into_x, into_dy):
    patch = points.shape[1]
    half = patch // 2
    first = pl.multiple_of(scal[1] * 128, 128)
    chosen = one_hot_rows(order[pl.ds(slot, 1), half * side:half * side + half], patch)
    x = mm(chosen, points[slot]).astype(BF16)
    into_dy[...] = mm(chosen, cotangent[slot]).astype(BF16)
    own[...] = x
    normed, unit, inverse = norm_half(x, gain[...], own[:, pl.ds(first, 128)])
    into_x[...] = normed
    return unit, inverse


def local_kernel(scal, order, points, cotangent, gain, gain_column, w3, wo,
                 send, keep, stats, unit_o, inv_o, wacc, wt, nrm_o, dy_o,
                 nrm, dy, own, *work):
    half = points.shape[1] // 2
    for t in range(3):
        wt[128 * t:128 * t + 128, :] = w3[t].astype(F32).T.astype(BF16)
    wacc[...] = jnp.zeros_like(wacc)

    def interior(p, carry):
        for side in range(2):
            rows = slice(half * side, half * side + half)
            unit, inverse = gather_rows(scal, order, points, cotangent, gain, own, p + side,
                                        1 - side, nrm.at[rows], dy.at[rows])
            unit_o[p, :, rows] = unit
            inv_o[p, :, rows] = inverse
        patch_core(scal[0], p, nrm, dy, w3, wt, wo, gain_column, send, keep, stats,
                   *work[:5], wacc, *work[5:])
        return carry

    lax.fori_loop(0, scal[2] - 1, interior, 0)

    @pl.when(scal[2] == 1)
    def _():
        for p in range(2):
            rows = slice(half * p, half * p + half)
            unit, inverse = gather_rows(scal, order, points, cotangent, gain, own, 0, 1 - p,
                                        nrm_o.at[p], dy_o.at[p])
            unit_o[p, :, rows] = unit
            inv_o[p, :, rows] = inverse


def cross_kernel(factor, scal, before, pull, pull_other, push, push_other, send_i, keep_i, stats_i,
                 unit_i, inv_i, wacc_i, nrm_i, dy_i, gain, gain_column, w3, wt, wo,
                 send, keep, stats, unit_o, inv_o, pieces, gain_o,
                 nrm, dy, own, *work_wacc):
    wacc, work = work_wacc[-1], work_wacc[:-1]
    half = nrm_i.shape[1]
    part = half // 2
    first = pl.multiple_of(scal[1] * 128, 128)
    light = scal[2] == 1
    stats[...] = stats_i[...]
    unit_o[...] = unit_i[...]
    inv_o[...] = inv_i[...]
    wacc[...] = wacc_i[...]

    def cross(p, carry):
        here = pl.multiple_of(half * p, half)
        there = pl.multiple_of(half * (1 - p), half)
        nrm[pl.ds(here, half), :] = nrm_i[p]
        dy[pl.ds(here, half), :] = dy_i[p]

        def take(one, other):
            for source, core in ((one, scal[0]), (other, 1 - scal[0])):
                at = pl.multiple_of(core * part, part)
                own[pl.ds(at, part), :] = source[0]
                dy[pl.ds(pl.multiple_of(there + at, part), part), :] = source[1]

        @pl.when(p == 0)
        def _():
            take(pull, pull_other)

        @pl.when(p == 1)
        def _():
            take(push, push_other)

        normed, unit, inverse = norm_half(own[...], gain[...], own[:, pl.ds(first, 128)])
        nrm[pl.ds(there, half), :] = normed
        unit_o[p, :, pl.ds(there, half)] = unit
        inv_o[p, :, pl.ds(there, half)] = inverse
        patch_core(scal[0], p, nrm, dy, w3, wt, wo, gain_column, send, keep, stats,
                   *work[:5], wacc, *work[5:])
        return carry

    lax.fori_loop(0, jnp.where(light, jnp.where(before[0] > 1, 2, 1), 0), cross, 0)
    total = wacc[0:384] * factor
    gain_o[...] = jnp.sum(total * wt[...].astype(F32), axis=0, keepdims=True) / gain[...]
    for r in range(16):
        for c in range(4):
            block = wacc[32 * r:32 * r + 32, 128 * c:128 * c + 128]
            pieces[4 * r + c] = (block * factor).astype(BF16)


def pair_kernel(scal, keep, received, stats, stats_received, send, kept, stats_o):
    far = scal[3]
    send[...] = (keep[1 - far].astype(F32) + received[1 - far].astype(F32)).astype(BF16)
    kept[...] = (keep[far].astype(F32) + received[far].astype(F32)).astype(BF16)
    stats_o[...] = stats[...] + stats_received[...]


def branch_kernel(scal, kept, received, stats, stats_received, unit, stat, gain_column,
                  branch, back, ahead):
    half = branch.shape[2] // 2
    own_gain = gain_column[pl.ds(pl.multiple_of(scal[1] * 128, 128), 128), :]
    scaled = (kept[...].astype(F32) + received[...].astype(F32)) * own_gain
    mean = (stats[0:1, :] + stats_received[0:1, :]) * (1.0 / D)
    slope = (stats[1:2, :] + stats_received[1:2, :]) * (1.0 / D)
    rows = (stat[0, 0:1, :] * (scaled - mean - unit[0].astype(F32) * slope)).astype(BF16)
    branch[0] = rows

    @pl.when(pl.program_id(0) == 0)
    def _():
        ahead[...] = rows[:, half:]

    @pl.when(pl.program_id(0) == 1)
    def _():
        back[...] = rows[:, :half]


def total_kernel(scal, received, gain, gain_received, out):
    def add(i, total):
        return total + received[i].astype(F32)

    total = lax.fori_loop(0, received.shape[0], add, jnp.zeros(received.shape[1:], F32), unroll=8)
    low = total.astype(BF16)
    at = pl.ds(pl.multiple_of(scal[1] * 128, 128), 128)
    own_gain = jnp.broadcast_to(gain[:, at] + gain_received[:, at], (8, 128)).astype(BF16)

    def put(i, carry):
        out[i, 0:32, :] = low
        out[i, 32:40, :] = own_gain
        return carry

    lax.fori_loop(0, received.shape[0], put, 0, unroll=8)


def place_kernel(scal, order, before, cotangent, branch, from_before, from_after, out, placed):
    slot = pl.program_id(0)
    count = scal[2]
    patch = out.shape[1]
    half = patch // 2

    @pl.when(slot >= count)
    def _():
        out[...] = cotangent[...]

    @pl.when(slot < count)
    def _():
        local = before[0] > 1

        @pl.when(jnp.logical_and(slot == 0, jnp.logical_not(local)))
        def _():
            placed[:, 0:half] = from_before[...]

        @pl.when(jnp.logical_and(slot == 0, local))
        def _():
            placed[:, 0:half] = branch[1, :, half:]

        @pl.when(slot > 0)
        def _():
            placed[:, 0:half] = branch[jnp.maximum(slot - 1, 0), :, half:]

        @pl.when(slot < 2)
        def _():
            placed[:, half:] = branch[jnp.minimum(slot, 1), :, 0:half]

        @pl.when(slot == 2)
        def _():
            placed[:, half:] = from_after[...]

        places = order[pl.ds(slot, 1), :]
        rows = 256
        for r in range(patch // rows):
            index = lax.broadcasted_iota(jnp.int32, (rows, patch), 0) + rows * r
            chosen = (index == places).astype(BF16)
            moved = mm_nt(chosen, placed[...])
            own = cotangent[0, rows * r:rows * r + rows, :].astype(F32)
            out[0, rows * r:rows * r + rows, :] = (own + moved).astype(BF16)


def finish_kernel(received, qkv, out, gain):
    gain[...] = jnp.sum(received[:, 32:40, :].astype(F32), axis=0)[0:1]
    for t in range(3):
        for c in range(4):
            block = jnp.concatenate(
                [received[4 * (4 * t + r) + c, 0:32, :].astype(F32) for r in range(4)], axis=0
            )
            qkv[t, 128 * c:128 * c + 128, :] = block.T
    for r in range(4):
        for c in range(4):
            out[32 * r:32 * r + 32, 128 * c:128 * c + 128] = received[
                4 * (12 + r) + c, 0:32, :
            ].astype(F32)


def shards(points, order, counts, cotangent, norm_gain, w_qkv, w_out):
    slots, patch, width = points.shape
    half = patch // 2
    curve = lax.axis_size("curve")
    model_part = lax.axis_index("mp")
    core = model_part % 2
    far = model_part // 2
    scal = jnp.stack([core, model_part, counts[0], far]).astype(jnp.int32)
    gain_row = norm_gain.reshape(1, width)
    gain_column = norm_gain.reshape(width, 1)
    w3 = jnp.transpose(w_qkv, (1, 0, 2))
    sds = jax.ShapeDtypeStruct

    def passed(x, by):
        return lax.ppermute(x, "curve", [(i, (i + by) % curve) for i in range(curve)])

    def swapped(x, bit):
        return lax.ppermute(x, "mp", [(i, i ^ bit) for i in range(4)])

    first_block = pl.BlockSpec((1, patch, width // 2), lambda i: (0, 0, i))
    last_block = pl.BlockSpec((1, patch, width // 2), lambda i: (slots - 1, 0, i))
    part_block = pl.BlockSpec((2, half // 2, width // 2), lambda i: (0, 0, i))
    pull, push = pl.pallas_call(
        halo_kernel,
        grid=(2,),
        in_specs=[SMEM, pl.BlockSpec((slots, patch), lambda i: (0, 0)),
                  first_block, first_block, last_block, last_block],
        out_specs=[part_block] * 2,
        out_shape=[sds((2, half // 2, width), BF16)] * 2,
        scratch_shapes=[pltpu.VMEM((2, half // 2, patch), BF16)],
        compiler_params=params(60),
        name="halo",
    )(scal, order, points, cotangent, points, cotangent)
    counts, pull = lax.optimization_barrier((counts, pull))
    before = passed(counts, 1)
    pull, push = passed(pull, -1), passed(push, 1)
    scal_local, before = lax.optimization_barrier((scal, before))

    work = [
        pltpu.VMEM((patch, width), BF16),
        pltpu.VMEM((patch, width), BF16),
        pltpu.VMEM((half, width), BF16),
        pltpu.VMEM((384, patch), BF16),
        pltpu.VMEM((patch, 128), BF16),
        pltpu.VMEM((patch, 128), BF16),
        pltpu.VMEM((128, patch), BF16),
        pltpu.VMEM((128, patch), BF16),
        pltpu.VMEM((384, patch), BF16),
        pltpu.VMEM((width, patch), BF16),
        pltpu.SemaphoreType.DMA((4,)),
    ]
    lanes = 2 * patch
    shared = [
        sds((2, 128, lanes), BF16),
        sds((2, 128, lanes), BF16),
        sds((2, lanes), F32),
        sds((2, 128, patch), BF16),
        sds((2, 8, patch), F32),
    ]
    send, keep, stats, unit, inverse, wacc, wt, nrm, dy = pl.pallas_call(
        local_kernel,
        in_specs=[SMEM] + [VMEM] * 7,
        out_specs=[ANY] * 2 + [VMEM] * 7,
        out_shape=shared + [
            sds((512, width), F32),
            sds((384, width), BF16),
            sds((2, half, width), BF16),
            sds((2, half, width), BF16),
        ],
        scratch_shapes=work,
        compiler_params=params(60),
        cost_estimate=cost(16 * 10**9, 16 * 10**6),
        name="local",
    )(scal_local, order, points, cotangent, gain_row, gain_column, w3, w_out)
    pull, push, wacc = lax.optimization_barrier((pull, push, wacc))

    factor = 1.0 / math.sqrt(curve * slots * patch)
    send, keep, stats, unit, inverse, pieces, gain_part = pl.pallas_call(
        functools.partial(cross_kernel, factor),
        in_specs=[SMEM] * 2 + [VMEM] * 4 + [ANY] * 2 + [VMEM] * 11,
        out_specs=[ANY] * 2 + [VMEM] * 5,
        out_shape=shared + [sds((64, 32, 128), BF16), sds((1, width), F32)],
        scratch_shapes=work + [pltpu.VMEM((512, width), F32)],
        input_output_aliases={6: 0, 7: 1},
        compiler_params=params(56),
        cost_estimate=cost(4 * 10**9, 8 * 10**6),
        name="cross",
    )(scal, before, pull, swapped(pull, 1), push, swapped(push, 1), send, keep, stats, unit,
      inverse, wacc, nrm, dy, gain_row, gain_column, w3, wt, w_out)

    received = lax.all_to_all(pieces, "curve", 0, 0)
    gain_part = gain_part + swapped(gain_part, 1)
    gain_far = swapped(gain_part, 2)

    def whole(*shape):
        return pl.BlockSpec(shape, lambda i: (0,) * len(shape))

    def by_patch(*shape):
        return pl.BlockSpec((1,) + shape, lambda i: (i,) + (0,) * len(shape))

    def by_lanes(*shape):
        return pl.BlockSpec(shape + (patch,), lambda i: (0,) * len(shape) + (i,))

    near, near_stats = swapped(send, 1), swapped(stats, 1)
    send, kept, stats = pl.pallas_call(
        pair_kernel,
        grid=(2,),
        in_specs=[SMEM, by_lanes(2, 128), by_lanes(2, 128), by_lanes(2), by_lanes(2)],
        out_specs=[by_lanes(128), by_lanes(128), by_lanes(2)],
        out_shape=[sds((128, lanes), BF16), sds((128, lanes), BF16), sds((2, lanes), F32)],
        compiler_params=params(16),
        cost_estimate=cost(1000, 1000),
        name="pair",
    )(scal, keep, near, stats, near_stats)
    send, gain_far = lax.optimization_barrier((send, gain_far))
    away, away_stats = swapped(send, 2), swapped(stats, 2)
    branch, back, ahead = pl.pallas_call(
        branch_kernel,
        grid=(2,),
        in_specs=[SMEM, by_lanes(128), by_lanes(128), by_lanes(2), by_lanes(2),
                  by_patch(128, patch), by_patch(8, patch), whole(width, 1)],
        out_specs=[by_patch(128, patch), whole(128, half), whole(128, half)],
        out_shape=[sds((2, 128, patch), BF16), sds((128, half), BF16), sds((128, half), BF16)],
        compiler_params=params(16),
        cost_estimate=cost(10**10, 1000),
        name="branch",
    )(scal, kept, away, stats, away_stats, unit, inverse, gain_column)
    from_before, from_after = passed(ahead, 1), passed(back, -1)

    totals = pl.pallas_call(
        total_kernel,
        in_specs=[SMEM] + [VMEM] * 3,
        out_specs=VMEM,
        out_shape=sds((64, 40, 128), BF16),
        compiler_params=params(16),
        name="total",
    )(scal, received, gain_part, gain_far)
    gathered = lax.all_to_all(totals, "curve", 0, 0)

    grad_points = pl.pallas_call(
        place_kernel,
        grid_spec=pltpu.PrefetchScalarGridSpec(
            num_scalar_prefetch=1,
            grid=(slots,),
            in_specs=[
                pl.BlockSpec((slots, patch), lambda i, s: (0, 0)),
                SMEM,
                pl.BlockSpec((1, patch, 128), lambda i, s: (i, 0, s[1])),
                pl.BlockSpec((2, 128, patch), lambda i, s: (0, 0, 0)),
                pl.BlockSpec((128, half), lambda i, s: (0, 0)),
                pl.BlockSpec((128, half), lambda i, s: (0, 0)),
            ],
            out_specs=pl.BlockSpec((1, patch, 128), lambda i, s: (i, 0, 0)),
            scratch_shapes=[pltpu.VMEM((128, patch), BF16)],
        ),
        out_shape=sds((slots, patch, 128), BF16),
        compiler_params=params(16),
        cost_estimate=cost(10**10, 1000),
        name="place",
    )(scal, order, before, cotangent, branch, from_before, from_after)

    grad_qkv, grad_out, grad_gain = pl.pallas_call(
        finish_kernel,
        in_specs=[VMEM],
        out_specs=[VMEM] * 3,
        out_shape=[sds((3, width, 128), F32), sds((128, width), F32), sds((1, 128), F32)],
        compiler_params=params(16),
        name="finish",
    )(gathered)
    return grad_points, grad_gain.reshape(128), jnp.transpose(grad_qkv, (1, 0, 2)), grad_out


def solution(mesh):
    in_specs = (
        P("curve", None, None),
        P("curve", None),
        P("curve"),
        P("curve", None, None),
        P(),
        P(None, None, "mp"),
        P("mp", None),
    )
    out_specs = (P("curve", None, "mp"), P("mp"), P(None, None, "mp"), P("mp", None))
    return jax.shard_map(shards, mesh=mesh, in_specs=in_specs, out_specs=out_specs, check_vma=False)
```

```python
import functools
import math

import jax
import jax.numpy as jnp
from jax import lax
from jax.experimental import pallas as pl
from jax.experimental.pallas import tpu as pltpu
from jax.sharding import PartitionSpec as P

D = 512
HEADS = 8
HEAD = D // HEADS
EPSILON = 1e-05
SCALE = HEAD ** (-0.5) * math.log2(math.e)

F32 = jnp.float32
BF16 = jnp.bfloat16
NT = (((1,), (1,)), ((), ()))
VMEM = pl.BlockSpec(memory_space=pltpu.VMEM)
SMEM = pl.BlockSpec(memory_space=pltpu.SMEM)
ANY = pl.BlockSpec(memory_space=pl.ANY)


def mm(a, b):
    return jnp.dot(a, b, preferred_element_type=F32)


def mm_nt(a, b):
    return lax.dot_general(a, b, NT, preferred_element_type=F32)


def params(mib):
    return pltpu.CompilerParams(vmem_limit_bytes=mib * 1024 * 1024)


def cost(flops, bytes_accessed):
    return pl.CostEstimate(flops=flops, bytes_accessed=bytes_accessed, transcendentals=0)


def one_hot_rows(places, patch):
    count = places.shape[1]
    column = jnp.broadcast_to(places, (128, count)).T
    lanes = lax.broadcasted_iota(jnp.int32, (count, 128), 1)
    return jnp.concatenate(
        [(column == lanes + 128 * b).astype(BF16) for b in range(patch // 128)], axis=1
    )


def halo_kernel(scal, order, points, cotangent, pull, push, held, done):
    rows = pull.shape[1]
    patch = points.shape[1]
    last = points.shape[0] - 1
    copies = []
    for slot in (last, 0):
        for source in (points, cotangent):
            k = len(copies)
            copies.append(pltpu.make_async_copy(source.at[slot], held.at[k], done.at[k]))
            copies[-1].start()
    count = jnp.zeros((16, push.shape[2]), F32) + scal[2].astype(F32)
    for k, (slot, base, out) in enumerate(((last, patch // 2, push), (0, 0, pull))):
        at = pl.ds(pl.multiple_of(base + scal[0] * rows, rows), rows)
        chosen = one_hot_rows(order[slot:slot + 1, at], patch)
        for j in range(2):
            copies[2 * k + j].wait()
            out[j, 0:rows, :] = mm(chosen, held[2 * k + j]).astype(BF16)
    push[0, rows:, :] = count.astype(BF16)
    push[1, rows:, :] = count.astype(BF16)


def norm_half(x, gain, own):
    values = x.astype(F32)
    mean = jnp.mean(values, axis=1, keepdims=True)
    centre = values - mean
    inverse = lax.rsqrt(jnp.mean(centre * centre, axis=1, keepdims=True) + EPSILON)
    normed = (centre * inverse * gain).astype(BF16)
    unit = ((own.astype(F32) - mean) * inverse).T.astype(BF16)
    inverse_row = jnp.broadcast_to(inverse, (x.shape[0], 128)).T[0:8]
    return normed, unit, inverse_row


def project(nrm, dy, weights, wt, wo, prj, kr, vr, dat):
    prj[0:128, :] = (mm_nt(wt[0:128, :], nrm[...]) * SCALE).astype(BF16)
    prj[128:384, :] = mm_nt(wt[128:384, :], nrm[...]).astype(BF16)
    both = mm(nrm[...], weights[0:D, 128:384]).astype(BF16)
    kr[...] = both[:, 0:128]
    vr[...] = both[:, 128:256]
    dat[...] = mm_nt(wo[...], dy[...]).astype(BF16)


def attend(prj, kr, vr, dat, gp, att, scores, lows):
    patch = prj.shape[1]
    chunk = 256
    blocks = [slice(c, c + chunk) for c in range(0, patch, chunk)]
    zeros = jnp.zeros((HEAD, patch), BF16)
    state = [{}, {}]

    def pad(x, h):
        return jnp.concatenate([x, zeros] if h == 0 else [zeros, x], axis=0)

    def fold(x, op):
        return op(x.reshape(chunk // 8, 8, patch), axis=0)

    def score(h, keys):
        here, lo = state[h], h * HEAD
        block = mm(kr[keys, :], pad(prj[lo:lo + HEAD, :], h))
        scores[h, keys, :] = block
        high = fold(block, jnp.max)
        here["high"] = jnp.maximum(here["high"], high) if "high" in here else high
        if keys.stop == patch:
            here["high"] = jnp.max(here["high"], axis=0, keepdims=True)

    def soften(h, keys):
        here, lo = state[h], h * HEAD
        expos = jnp.exp2(scores[h, keys, :] - here["high"])
        scores[h, keys, :] = expos
        lows[h, keys, :] = expos.astype(BF16)
        total = fold(expos, jnp.sum)
        here["total"] = here["total"] + total if "total" in here else total
        if keys.stop == patch:
            recip = 1.0 / jnp.sum(here["total"], axis=0, keepdims=True)
            attended = mm(prj[256 + lo:256 + lo + HEAD, :], lows[h]) * recip
            att[lo:lo + HEAD, :] = attended.astype(BF16)
            grad = dat[lo:lo + HEAD, :].astype(F32) * recip
            here["inner"] = jnp.sum(grad * attended, axis=0, keepdims=True)
            here["grad"] = grad.astype(BF16)

    def back(h, keys):
        here, lo = state[h], h * HEAD
        grad_probs = mm(vr[keys, :], pad(here["grad"], h))
        grad_scores = (scores[h, keys, :] * (grad_probs - here["inner"])).astype(BF16)
        dk = mm_nt(prj[lo:lo + HEAD, :], grad_scores) * (HEAD ** (-0.5) / SCALE)
        gp[128 + lo:128 + lo + HEAD, keys] = dk.astype(BF16)
        gp[256 + lo:256 + lo + HEAD, keys] = mm_nt(here["grad"], lows[h, keys, :]).astype(BF16)
        lows[h, keys, :] = grad_scores
        if keys.stop == patch:
            dq = mm(prj[128 + lo:128 + lo + HEAD, :], lows[h]) * (HEAD ** (-0.5))
            gp[lo:lo + HEAD, :] = dq.astype(BF16)

    for keys in blocks:
        score(0, keys)
    for keys in blocks:
        score(1, keys)
        soften(0, keys)
    for keys in blocks:
        back(0, keys)
        soften(1, keys)
    for keys in blocks:
        back(1, keys)


def split3(x):
    first = x.astype(BF16)
    rest = x - first.astype(F32)
    second = rest.astype(BF16)
    third = (rest - second.astype(F32)).astype(BF16)
    none = jnp.zeros((13, x.shape[1]), BF16)
    return jnp.concatenate([first, second, third, none], axis=0)


def load_weights(w3, wt, gain, weights):
    for t in range(3):
        weights[0:D, 128 * t:128 * t + 128] = w3[t]
    sums = jnp.sum(mm_nt(split3(gain[...]), wt[...]), axis=0, keepdims=True)
    weights[D:D + 16, :] = split3(sums)


def patch_core(core, p, nrm, dy, wt, wo, send, keep, stats, wacc,
               prj, kr, vr, dat, att, gp, grads, scores, lows, weights, done):
    project(nrm, dy, weights, wt, wo, prj, kr, vr, dat)
    attend(prj, kr, vr, dat, gp, att, scores, lows)
    patch = gp.shape[1]
    cols = pl.ds(pl.multiple_of(p * patch, patch), patch)
    grads[...] = mm(weights[0:D, :], gp[...]).astype(BF16)
    copies = []
    for j in range(2):
        for k, (block, into) in enumerate(((2 * j + 1 - core, send), (2 * j + core, keep))):
            rows = pl.ds(pl.multiple_of(block * 128, 128), 128)
            copies.append(
                pltpu.make_async_copy(grads.at[rows], into.at[j, :, cols], done.at[2 * j + k])
            )
            copies[-1].start()
    wacc[0:384] += mm(gp[...], nrm[...])
    wacc[384:512] += mm(att[...], dy[...])
    stats[0:1, cols] = jnp.sum(mm(weights[D:D + 16, :], gp[...]), axis=0, keepdims=True)
    stats[1:2, cols] = second_stat(gp, prj)
    for copy in copies:
        copy.wait()


def second_stat(gp, prj):
    product = gp[...].astype(F32) * prj[...].astype(F32)
    queries = jnp.sum(product[0:128], axis=0, keepdims=True) * (1.0 / SCALE)
    return queries + jnp.sum(product[128:384], axis=0, keepdims=True)


def gather_rows(scal, order, points, cotangent, gain, own, slot, side, into_x, into_dy):
    patch = points.shape[1]
    half = patch // 2
    first = pl.multiple_of(scal[1] * 128, 128)
    chosen = one_hot_rows(order[pl.ds(slot, 1), half * side:half * side + half], patch)
    x = mm(chosen, points[slot]).astype(BF16)
    into_dy[...] = mm(chosen, cotangent[slot]).astype(BF16)
    own[...] = x
    normed, unit, inverse = norm_half(x, gain[...], own[:, pl.ds(first, 128)])
    into_x[...] = normed
    return unit, inverse


def local_kernel(scal, order, points, cotangent, gain, w3, wo,
                 send, keep, stats, unit_o, inv_o, wacc, wt, nrm_o, dy_o,
                 nrm, dy, own, *work):
    half = points.shape[1] // 2
    for t in range(3):
        wt[128 * t:128 * t + 128, :] = w3[t].astype(F32).T.astype(BF16)
    wacc[...] = jnp.zeros_like(wacc)
    load_weights(w3, wt, gain, work[-2])

    whole = scal[2] > 1

    def step(p, carry):
        for side in range(2):
            rows = slice(half * side, half * side + half)

            @pl.when(jnp.logical_or(whole, p == side))
            def _():
                slot = jnp.where(whole, p + side, 0)
                unit, inverse = gather_rows(scal, order, points, cotangent, gain, own, slot,
                                            1 - side, nrm.at[rows], dy.at[rows])
                unit_o[p, :, rows] = unit
                inv_o[p, :, rows] = inverse

        @pl.when(whole)
        def _():
            patch_core(scal[0], p, nrm, dy, wt, wo, send, keep, stats, wacc, *work)

        @pl.when(jnp.logical_not(whole))
        def _():
            here = pl.ds(pl.multiple_of(half * p, half), half)
            nrm_o[p] = nrm[here, :]
            dy_o[p] = dy[here, :]

        return carry

    lax.fori_loop(0, 2, step, 0)


def cross_kernel(factor, scal, pull, pull_other, push, push_other, send_i, keep_i, wacc_i, nrm_i,
                 dy_i, stats_i, unit_i, inv_i, gain, w3, wt, wo,
                 send, keep, stats, unit_o, inv_o, pieces, gain_o, pushed,
                 flag, nrm_2, dy_2, own_2, arrived, *work_wacc):
    wacc, work = work_wacc[-1], work_wacc[:-1]
    half = nrm_i.shape[1]
    part = half // 2
    first = pl.multiple_of(scal[1] * 128, 128)
    light = scal[2] == 1
    told = pltpu.make_async_copy(push.at[0, part:part + 16], flag, arrived.at[2, 0])
    told.start()
    copies = []
    for p, one, other in ((0, pull, pull_other), (1, push, push_other)):
        here, there = half * p, half * (1 - p)
        moves = [(nrm_i.at[p], nrm_2.at[p, here:here + half]),
                 (dy_i.at[p], dy_2.at[p, here:here + half])]
        for source, core in ((one, scal[0]), (other, 1 - scal[0])):
            at = pl.multiple_of(core * part, part)
            moves.append((source.at[0, 0:part], own_2.at[p, pl.ds(at, part)]))
            moves.append((source.at[1, 0:part],
                          dy_2.at[p, pl.ds(pl.multiple_of(there + at, part), part)]))
        copies.append([pltpu.make_async_copy(source, into, arrived.at[p, k])
                       for k, (source, into) in enumerate(moves)])
        for copy in copies[-1]:
            copy.start()
    stats[...] = stats_i[...]
    unit_o[...] = unit_i[...]
    inv_o[...] = inv_i[...]
    load_weights(w3, wt, gain, work[-2])

    @pl.when(light)
    def _():
        wacc[...] = jnp.zeros_like(wacc)

    @pl.when(jnp.logical_not(light))
    def _():
        copy = pltpu.make_async_copy(wacc_i, wacc, work[-1].at[0])
        copy.start()
        copy.wait()

    told.wait()
    before = jnp.max(flag[...].astype(F32)).astype(jnp.int32)
    pushed[0] = before
    patches = jnp.where(light, jnp.where(before > 1, 2, 1), 0)

    def cross(p, carry):
        for q in range(2):
            @pl.when(p == q)
            def _():
                for copy in copies[q]:
                    copy.wait()

        @pl.when(p < patches)
        def _():
            there = pl.multiple_of(half * (1 - p), half)
            own = own_2.at[p]
            nrm = nrm_2.at[p]
            normed, unit, inverse = norm_half(own[...], gain[...], own[:, pl.ds(first, 128)])
            nrm[pl.ds(there, half), :] = normed
            unit_o[p, :, pl.ds(there, half)] = unit
            inv_o[p, :, pl.ds(there, half)] = inverse
            patch_core(scal[0], p, nrm, dy_2.at[p], wt, wo, send, keep, stats, wacc, *work)

        return carry

    lax.fori_loop(0, 2, cross, 0)
    total = wacc[0:384] * factor
    gain_o[...] = jnp.sum(total * wt[...].astype(F32), axis=0, keepdims=True) / gain[...]
    for r in range(16):
        for c in range(4):
            block = wacc[32 * r:32 * r + 32, 128 * c:128 * c + 128]
            pieces[4 * r + c] = (block * factor).astype(BF16)


def pair_kernel(scal, keep, received, stats, stats_received, send, kept, stats_o):
    far = scal[3]
    send[...] = (keep[1 - far].astype(F32) + received[1 - far].astype(F32)).astype(BF16)
    kept[...] = (keep[far].astype(F32) + received[far].astype(F32)).astype(BF16)
    stats_o[...] = stats[...] + stats_received[...]


def branch_kernel(scal, kept, received, stats, stats_received, unit, stat, gain,
                  branch, back, ahead):
    half = branch.shape[2] // 2
    own_gain = gain[:, pl.ds(pl.multiple_of(scal[1] * 128, 128), 128)]
    own_gain = jnp.broadcast_to(own_gain, (128, 128)).T[:, 0:1]
    scaled = (kept[...].astype(F32) + received[...].astype(F32)) * own_gain
    mean = (stats[0:1, :] + stats_received[0:1, :]) * (1.0 / D)
    slope = (stats[1:2, :] + stats_received[1:2, :]) * (1.0 / D)
    rows = (stat[0, 0:1, :] * (scaled - mean - unit[0].astype(F32) * slope)).astype(BF16)
    branch[0] = rows

    @pl.when(pl.program_id(0) == 0)
    def _():
        ahead[...] = rows[:, half:]

    @pl.when(pl.program_id(0) == 1)
    def _():
        back[...] = rows[:, :half]


def total_kernel(scal, received, gain, gain_received, out):
    def add(i, total):
        return total + received[i].astype(F32)

    total = lax.fori_loop(0, received.shape[0], add, jnp.zeros(received.shape[1:], F32), unroll=8)
    low = total.astype(BF16)
    at = pl.ds(pl.multiple_of(scal[1] * 128, 128), 128)
    own_gain = jnp.broadcast_to(gain[:, at] + gain_received[:, at], (8, 128)).astype(BF16)

    def put(i, carry):
        out[i, 0:32, :] = low
        out[i, 32:40, :] = own_gain
        return carry

    lax.fori_loop(0, received.shape[0], put, 0, unroll=8)


def place_kernel(scal, order, before, cotangent, branch, from_before, from_after, out, placed):
    slot = pl.program_id(0)
    count = scal[2]
    patch = out.shape[1]
    half = patch // 2

    @pl.when(slot >= count)
    def _():
        out[...] = cotangent[...]

    @pl.when(slot < count)
    def _():
        local = before[0] > 1

        @pl.when(jnp.logical_and(slot == 0, jnp.logical_not(local)))
        def _():
            placed[:, 0:half] = from_before[...]

        @pl.when(jnp.logical_and(slot == 0, local))
        def _():
            placed[:, 0:half] = branch[1, :, half:]

        @pl.when(slot > 0)
        def _():
            placed[:, 0:half] = branch[jnp.maximum(slot - 1, 0), :, half:]

        @pl.when(slot < 2)
        def _():
            placed[:, half:] = branch[jnp.minimum(slot, 1), :, 0:half]

        @pl.when(slot == 2)
        def _():
            placed[:, half:] = from_after[...]

        places = order[pl.ds(slot, 1), :]
        rows = 256
        for r in range(patch // rows):
            index = lax.broadcasted_iota(jnp.int32, (rows, patch), 0) + rows * r
            chosen = (index == places).astype(BF16)
            moved = mm_nt(chosen, placed[...])
            own = cotangent[0, rows * r:rows * r + rows, :].astype(F32)
            out[0, rows * r:rows * r + rows, :] = (own + moved).astype(BF16)


def finish_kernel(received, qkv, out, gain):
    gain[...] = jnp.sum(received[:, 32:40, :].astype(F32), axis=0)[0:1]
    for t in range(3):
        for c in range(4):
            block = jnp.concatenate(
                [received[4 * (4 * t + r) + c, 0:32, :].astype(F32) for r in range(4)], axis=0
            )
            qkv[t, 128 * c:128 * c + 128, :] = block.T
    for r in range(4):
        for c in range(4):
            out[32 * r:32 * r + 32, 128 * c:128 * c + 128] = received[
                4 * (12 + r) + c, 0:32, :
            ].astype(F32)


def shards(points, order, counts, cotangent, norm_gain, w_qkv, w_out):
    slots, patch, width = points.shape
    half = patch // 2
    curve = lax.axis_size("curve")
    model_part = lax.axis_index("mp")
    core = model_part % 2
    far = model_part // 2
    scal = jnp.stack([core, model_part, counts[0], far]).astype(jnp.int32)
    gain_row = norm_gain.reshape(1, width)
    w3 = jnp.transpose(w_qkv, (1, 0, 2))
    sds = jax.ShapeDtypeStruct

    def passed(x, by):
        return lax.ppermute(x, "curve", [(i, (i + by) % curve) for i in range(curve)])

    def swapped(x, bit):
        return lax.ppermute(x, "mp", [(i, i ^ bit) for i in range(4)])

    pull, push = pl.pallas_call(
        halo_kernel,
        in_specs=[SMEM, VMEM, ANY, ANY],
        out_specs=[VMEM] * 2,
        out_shape=[sds((2, half // 2, width), BF16), sds((2, half // 2 + 16, width), BF16)],
        scratch_shapes=[pltpu.VMEM((4, patch, width), BF16), pltpu.SemaphoreType.DMA((4,))],
        compiler_params=params(60),
        name="halo",
    )(scal, order, points, cotangent)
    pull, push = passed(pull, -1), passed(push, 1)

    rows = [
        pltpu.VMEM((patch, width), BF16),
        pltpu.VMEM((patch, width), BF16),
        pltpu.VMEM((half, width), BF16),
    ]
    rows_2 = [
        pltpu.VMEM((16, width), BF16),
        pltpu.VMEM((2, patch, width), BF16),
        pltpu.VMEM((2, patch, width), BF16),
        pltpu.VMEM((2, half, width), BF16),
        pltpu.SemaphoreType.DMA((3, 6)),
    ]
    work = [
        pltpu.VMEM((384, patch), BF16),
        pltpu.VMEM((patch, 128), BF16),
        pltpu.VMEM((patch, 128), BF16),
        pltpu.VMEM((128, patch), BF16),
        pltpu.VMEM((128, patch), BF16),
        pltpu.VMEM((384, patch), BF16),
        pltpu.VMEM((width, patch), BF16),
        pltpu.VMEM((2, patch, patch), F32),
        pltpu.VMEM((2, patch, patch), BF16),
        pltpu.VMEM((width + 16, 384), BF16),
        pltpu.SemaphoreType.DMA((4,)),
    ]
    lanes = 2 * patch
    shared = [
        sds((2, 128, lanes), BF16),
        sds((2, 128, lanes), BF16),
        sds((2, lanes), F32),
        sds((2, 128, patch), BF16),
        sds((2, 8, patch), F32),
    ]
    send, keep, stats, unit, inverse, wacc, wt, nrm, dy = pl.pallas_call(
        local_kernel,
        in_specs=[SMEM] + [VMEM] * 6,
        out_specs=[ANY] * 2 + [VMEM] * 7,
        out_shape=shared + [
            sds((512, width), F32),
            sds((384, width), BF16),
            sds((2, half, width), BF16),
            sds((2, half, width), BF16),
        ],
        scratch_shapes=rows + work,
        compiler_params=params(60),
        cost_estimate=cost(16 * 10**9, 16 * 10**6),
        name="local",
    )(scal, order, points, cotangent, gain_row, w3, w_out)
    pull, push, wacc = lax.optimization_barrier((pull, push, wacc))

    factor = 1.0 / math.sqrt(curve * slots * patch)
    send, keep, stats, unit, inverse, pieces, gain_part, before = pl.pallas_call(
        functools.partial(cross_kernel, factor),
        in_specs=[SMEM] + [ANY] * 9 + [VMEM] * 7,
        out_specs=[ANY] * 2 + [VMEM] * 5 + [SMEM],
        out_shape=shared + [
            sds((64, 32, 128), BF16), sds((1, width), F32), sds((1,), jnp.int32)
        ],
        scratch_shapes=rows_2 + work + [pltpu.VMEM((512, width), F32)],
        input_output_aliases={5: 0, 6: 1},
        compiler_params=params(60),
        cost_estimate=cost(4 * 10**9, 8 * 10**6),
        name="cross",
    )(scal, pull, swapped(pull, 1), push, swapped(push, 1), send, keep, wacc, nrm, dy, stats, unit,
      inverse, gain_row, w3, wt, w_out)

    received = lax.all_to_all(pieces, "curve", 0, 0)
    gain_part = gain_part + swapped(gain_part, 1)
    gain_far = swapped(gain_part, 2)

    def whole(*shape):
        return pl.BlockSpec(shape, lambda i: (0,) * len(shape))

    def by_patch(*shape):
        return pl.BlockSpec((1,) + shape, lambda i: (i,) + (0,) * len(shape))

    def by_lanes(*shape):
        return pl.BlockSpec(shape + (patch,), lambda i: (0,) * len(shape) + (i,))

    near, near_stats = swapped(send, 1), swapped(stats, 1)
    send, kept, stats = pl.pallas_call(
        pair_kernel,
        grid=(2,),
        in_specs=[SMEM, by_lanes(2, 128), by_lanes(2, 128), by_lanes(2), by_lanes(2)],
        out_specs=[by_lanes(128), by_lanes(128), by_lanes(2)],
        out_shape=[sds((128, lanes), BF16), sds((128, lanes), BF16), sds((2, lanes), F32)],
        compiler_params=params(16),
        cost_estimate=cost(1000, 1000),
        name="pair",
    )(scal, keep, near, stats, near_stats)
    send, gain_far = lax.optimization_barrier((send, gain_far))
    away, away_stats = swapped(send, 2), swapped(stats, 2)
    branch, back, ahead = pl.pallas_call(
        branch_kernel,
        grid=(2,),
        in_specs=[SMEM, by_lanes(128), by_lanes(128), by_lanes(2), by_lanes(2),
                  by_patch(128, patch), by_patch(8, patch), whole(1, width)],
        out_specs=[by_patch(128, patch), whole(128, half), whole(128, half)],
        out_shape=[sds((2, 128, patch), BF16), sds((128, half), BF16), sds((128, half), BF16)],
        compiler_params=params(16),
        cost_estimate=cost(10**10, 1000),
        name="branch",
    )(scal, kept, away, stats, away_stats, unit, inverse, gain_row)
    from_before, from_after = passed(ahead, 1), passed(back, -1)

    totals = pl.pallas_call(
        total_kernel,
        in_specs=[SMEM] + [VMEM] * 3,
        out_specs=VMEM,
        out_shape=sds((64, 40, 128), BF16),
        compiler_params=params(16),
        name="total",
    )(scal, received, gain_part, gain_far)
    gathered = lax.all_to_all(totals, "curve", 0, 0)

    grad_points = pl.pallas_call(
        place_kernel,
        grid_spec=pltpu.PrefetchScalarGridSpec(
            num_scalar_prefetch=1,
            grid=(slots,),
            in_specs=[
                pl.BlockSpec((slots, patch), lambda i, s: (0, 0)),
                SMEM,
                pl.BlockSpec((1, patch, 128), lambda i, s: (i, 0, s[1])),
                pl.BlockSpec((2, 128, patch), lambda i, s: (0, 0, 0)),
                pl.BlockSpec((128, half), lambda i, s: (0, 0)),
                pl.BlockSpec((128, half), lambda i, s: (0, 0)),
            ],
            out_specs=pl.BlockSpec((1, patch, 128), lambda i, s: (i, 0, 0)),
            scratch_shapes=[pltpu.VMEM((128, patch), BF16)],
        ),
        out_shape=sds((slots, patch, 128), BF16),
        compiler_params=params(16),
        cost_estimate=cost(10**10, 1000),
        name="place",
    )(scal, order, before, cotangent, branch, from_before, from_after)

    grad_qkv, grad_out, grad_gain = pl.pallas_call(
        finish_kernel,
        in_specs=[VMEM],
        out_specs=[VMEM] * 3,
        out_shape=[sds((3, width, 128), F32), sds((128, width), F32), sds((1, 128), F32)],
        compiler_params=params(16),
        name="finish",
    )(gathered)
    return grad_points, grad_gain.reshape(128), jnp.transpose(grad_qkv, (1, 0, 2)), grad_out


def solution(mesh):
    in_specs = (
        P("curve", None, None),
        P("curve", None),
        P("curve"),
        P("curve", None, None),
        P(),
        P(None, None, "mp"),
        P("mp", None),
    )
    out_specs = (P("curve", None, "mp"), P("mp"), P(None, None, "mp"), P("mp", None))
    return jax.shard_map(shards, mesh=mesh, in_specs=in_specs, out_specs=out_specs, check_vma=False)
```

```python
import functools
import math

import jax
import jax.numpy as jnp
from jax import lax
from jax.experimental import pallas as pl
from jax.experimental.pallas import tpu as pltpu
from jax.sharding import PartitionSpec as P

D = 512
HEADS = 8
HEAD = D // HEADS
EPSILON = 1e-05
SCALE = HEAD ** (-0.5) * math.log2(math.e)

F32 = jnp.float32
BF16 = jnp.bfloat16
NT = (((1,), (1,)), ((), ()))
VMEM = pl.BlockSpec(memory_space=pltpu.VMEM)
SMEM = pl.BlockSpec(memory_space=pltpu.SMEM)
ANY = pl.BlockSpec(memory_space=pl.ANY)
HBM = pl.BlockSpec(memory_space=pltpu.HBM)


def mm(a, b):
    return jnp.dot(a, b, preferred_element_type=F32)


def mm_nt(a, b):
    return lax.dot_general(a, b, NT, preferred_element_type=F32)


def params(mib):
    return pltpu.CompilerParams(vmem_limit_bytes=mib * 1024 * 1024)


def cost(flops, bytes_accessed):
    return pl.CostEstimate(flops=flops, bytes_accessed=bytes_accessed, transcendentals=0)


def one_hot_rows(places, patch):
    count = places.shape[1]
    column = jnp.broadcast_to(places, (128, count)).T
    lanes = lax.broadcasted_iota(jnp.int32, (count, 128), 1)
    return jnp.concatenate(
        [(column == lanes + 128 * b).astype(BF16) for b in range(patch // 128)], axis=1
    )


def halo_kernel(counts, order_i, points, cotangent, pull, push, order, held, done):
    rows = pull.shape[1]
    patch = points.shape[1]
    last = points.shape[0] - 1
    core = lax.axis_index("mp") % 2
    places = pltpu.make_async_copy(order_i, order, done.at[4])
    places.start()
    copies = []
    for slot in (last, 0):
        for source in (points, cotangent):
            k = len(copies)
            copies.append(pltpu.make_async_copy(source.at[slot], held.at[k], done.at[k]))
            copies[-1].start()
    count = jnp.zeros((16, push.shape[2]), F32) + counts[0].astype(F32)
    push[0, rows:, :] = count.astype(BF16)
    push[1, rows:, :] = count.astype(BF16)
    places.wait()
    for k, (slot, base, out) in enumerate(((last, patch // 2, push), (0, 0, pull))):
        at = pl.ds(pl.multiple_of(base + core * rows, rows), rows)
        chosen = one_hot_rows(order[slot:slot + 1, at], patch)
        for j in range(2):
            copies[2 * k + j].wait()
            out[j, 0:rows, :] = mm(chosen, held[2 * k + j]).astype(BF16)


def norm_half(x, gain, own):
    values = x.astype(F32)
    mean = jnp.mean(values, axis=1, keepdims=True)
    centre = values - mean
    inverse = lax.rsqrt(jnp.mean(centre * centre, axis=1, keepdims=True) + EPSILON)
    normed = (centre * inverse * gain).astype(BF16)
    unit = ((own.astype(F32) - mean) * inverse).T.astype(BF16)
    inverse_row = jnp.broadcast_to(inverse, (x.shape[0], 128)).T[0:8]
    return normed, unit, inverse_row


def project(nrm, dy, weights, wt, wo, prj, kr, vr, dat):
    prj[0:128, :] = (mm_nt(wt[0:128, :], nrm[...]) * SCALE).astype(BF16)
    prj[128:384, :] = mm_nt(wt[128:384, :], nrm[...]).astype(BF16)
    both = mm(nrm[...], weights[0:D, 128:384]).astype(BF16)
    kr[...] = both[:, 0:128]
    vr[...] = both[:, 128:256]
    dat[...] = mm_nt(wo[...], dy[...]).astype(BF16)


def attend(prj, kr, vr, dat, gp, att, scores, lows):
    patch = prj.shape[1]
    chunk = 256
    blocks = [slice(c, c + chunk) for c in range(0, patch, chunk)]
    zeros = jnp.zeros((HEAD, patch), BF16)
    state = [{}, {}]

    def pad(x, h):
        return jnp.concatenate([x, zeros] if h == 0 else [zeros, x], axis=0)

    def fold(x, op):
        return op(x.reshape(chunk // 8, 8, patch), axis=0)

    def score(h, keys):
        here, lo = state[h], h * HEAD
        block = mm(kr[keys, :], pad(prj[lo:lo + HEAD, :], h))
        scores[h, keys, :] = block
        high = fold(block, jnp.max)
        here["high"] = jnp.maximum(here["high"], high) if "high" in here else high
        if keys.stop == patch:
            here["high"] = jnp.max(here["high"], axis=0, keepdims=True)

    def soften(h, keys):
        here, lo = state[h], h * HEAD
        expos = jnp.exp2(scores[h, keys, :] - here["high"])
        scores[h, keys, :] = expos
        lows[h, keys, :] = expos.astype(BF16)
        total = fold(expos, jnp.sum)
        here["total"] = here["total"] + total if "total" in here else total
        if keys.stop == patch:
            recip = 1.0 / jnp.sum(here["total"], axis=0, keepdims=True)
            attended = mm(prj[256 + lo:256 + lo + HEAD, :], lows[h]) * recip
            att[lo:lo + HEAD, :] = attended.astype(BF16)
            grad = dat[lo:lo + HEAD, :].astype(F32) * recip
            here["inner"] = jnp.sum(grad * attended, axis=0, keepdims=True)
            here["grad"] = grad.astype(BF16)

    def back(h, keys):
        here, lo = state[h], h * HEAD
        grad_probs = mm(vr[keys, :], pad(here["grad"], h))
        grad_scores = (scores[h, keys, :] * (grad_probs - here["inner"])).astype(BF16)
        dk = mm_nt(prj[lo:lo + HEAD, :], grad_scores) * (HEAD ** (-0.5) / SCALE)
        gp[128 + lo:128 + lo + HEAD, keys] = dk.astype(BF16)
        gp[256 + lo:256 + lo + HEAD, keys] = mm_nt(here["grad"], lows[h, keys, :]).astype(BF16)
        lows[h, keys, :] = grad_scores
        if keys.stop == patch:
            dq = mm(prj[128 + lo:128 + lo + HEAD, :], lows[h]) * (HEAD ** (-0.5))
            gp[lo:lo + HEAD, :] = dq.astype(BF16)

    for keys in blocks:
        score(0, keys)
    for keys in blocks:
        score(1, keys)
        soften(0, keys)
    for keys in blocks:
        back(0, keys)
        soften(1, keys)
    for keys in blocks:
        back(1, keys)


def split3(x):
    first = x.astype(BF16)
    rest = x - first.astype(F32)
    second = rest.astype(BF16)
    third = (rest - second.astype(F32)).astype(BF16)
    none = jnp.zeros((13, x.shape[1]), BF16)
    return jnp.concatenate([first, second, third, none], axis=0)


def load_weights(w3, wt, gain, weights):
    for t in range(3):
        weights[0:D, 128 * t:128 * t + 128] = w3[t]
    sums = jnp.sum(mm_nt(split3(gain[...]), wt[...]), axis=0, keepdims=True)
    weights[D:D + 16, :] = split3(sums)


def patch_core(core, p, nrm, dy, weights, wt, wo, send, keep, stats, wacc,
               prj, kr, vr, dat, att, gp, grads, scores, lows, done):
    project(nrm, dy, weights, wt, wo, prj, kr, vr, dat)
    attend(prj, kr, vr, dat, gp, att, scores, lows)
    patch = gp.shape[1]
    cols = pl.ds(pl.multiple_of(p * patch, patch), patch)
    grads[...] = mm(weights[0:D, :], gp[...]).astype(BF16)
    copies = []
    for j in range(2):
        for k, (block, into) in enumerate(((2 * j + 1 - core, send), (2 * j + core, keep))):
            rows = pl.ds(pl.multiple_of(block * 128, 128), 128)
            copies.append(
                pltpu.make_async_copy(grads.at[rows], into.at[j, :, cols], done.at[2 * j + k])
            )
            copies[-1].start()
    wacc[0:384] += mm(gp[...], nrm[...])
    wacc[384:512] += mm(att[...], dy[...])
    stats[0:1, cols] = jnp.sum(mm(weights[D:D + 16, :], gp[...]), axis=0, keepdims=True)
    stats[1:2, cols] = second_stat(gp, prj)
    for copy in copies:
        copy.wait()


def second_stat(gp, prj):
    product = gp[...].astype(F32) * prj[...].astype(F32)
    queries = jnp.sum(product[0:128], axis=0, keepdims=True) * (1.0 / SCALE)
    return queries + jnp.sum(product[128:384], axis=0, keepdims=True)


def gather_rows(scal, order, points, cotangent, gain, own, slot, side, into_x, into_dy):
    patch = points.shape[1]
    half = patch // 2
    first = pl.multiple_of(scal[1] * 128, 128)
    chosen = one_hot_rows(order[pl.ds(slot, 1), half * side:half * side + half], patch)
    x = mm(chosen, points[slot]).astype(BF16)
    into_dy[...] = mm(chosen, cotangent[slot]).astype(BF16)
    own[...] = x
    normed, unit, inverse = norm_half(x, gain[...], own[:, pl.ds(first, 128)])
    into_x[...] = normed
    return unit, inverse


def local_kernel(scal, order, points, cotangent, gain, w3, wo,
                 send, keep, stats, unit_o, inv_o, wacc, weights, wt, nrm_o, dy_o,
                 nrm, dy, own, *work):
    half = points.shape[1] // 2
    for t in range(3):
        wt[128 * t:128 * t + 128, :] = w3[t].astype(F32).T.astype(BF16)
    wacc[...] = jnp.zeros_like(wacc)
    load_weights(w3, wt, gain, weights)

    whole = scal[2] > 1

    def step(p, carry):
        for side in range(2):
            rows = slice(half * side, half * side + half)

            @pl.when(jnp.logical_or(whole, p == side))
            def _():
                slot = jnp.where(whole, p + side, 0)
                unit, inverse = gather_rows(scal, order, points, cotangent, gain, own, slot,
                                            1 - side, nrm.at[rows], dy.at[rows])
                unit_o[p, :, rows] = unit
                inv_o[p, :, rows] = inverse

        @pl.when(whole)
        def _():
            patch_core(scal[0], p, nrm, dy, weights, wt, wo, send, keep, stats, wacc, *work)

        @pl.when(jnp.logical_not(whole))
        def _():
            here = pl.ds(pl.multiple_of(half * p, half), half)
            nrm_o[p] = nrm[here, :]
            dy_o[p] = dy[here, :]

        return carry

    lax.fori_loop(0, 2, step, 0)


def cross_kernel(factor, scal, pull, pull_other, push, push_other, send_i, keep_i, wacc_i, nrm_i,
                 dy_i, stats_i, unit_i, inv_i, weights_i, wt_i, wo_i, gain,
                 send, keep, stats, unit_o, inv_o, pieces, gain_o, pushed,
                 flag, nrm_2, dy_2, own_2, weights, wt, wo, arrived, *work_wacc):
    wacc, work = work_wacc[-1], work_wacc[:-1]
    half = nrm_i.shape[1]
    part = half // 2
    first = pl.multiple_of(scal[1] * 128, 128)
    light = scal[2] == 1
    told = pltpu.make_async_copy(push.at[0, part:part + 16], flag, arrived.at[2, 0])
    told.start()
    copies = []
    common = ((stats_i, stats), (unit_i, unit_o), (inv_i, inv_o), (weights_i, weights), (wt_i, wt),
              (wo_i, wo))
    common = [pltpu.make_async_copy(source, into, arrived.at[2, k + 1])
              for k, (source, into) in enumerate(common)]
    for p, one, other in ((0, pull, pull_other), (1, push, push_other)):
        here, there = half * p, half * (1 - p)
        moves = [(nrm_i.at[p], nrm_2.at[p, here:here + half]),
                 (dy_i.at[p], dy_2.at[p, here:here + half])]
        for source, core in ((one, scal[0]), (other, 1 - scal[0])):
            at = pl.multiple_of(core * part, part)
            moves.append((source.at[0, 0:part], own_2.at[p, pl.ds(at, part)]))
            moves.append((source.at[1, 0:part],
                          dy_2.at[p, pl.ds(pl.multiple_of(there + at, part), part)]))
        copies.append([pltpu.make_async_copy(source, into, arrived.at[p, k])
                       for k, (source, into) in enumerate(moves)])
        for copy in copies[-1]:
            copy.start()
        if p == 0:
            for copy in common:
                copy.start()
    @pl.when(light)
    def _():
        wacc[...] = jnp.zeros_like(wacc)

    @pl.when(jnp.logical_not(light))
    def _():
        copy = pltpu.make_async_copy(wacc_i, wacc, work[-1].at[0])
        copy.start()
        copy.wait()

    told.wait()
    for copy in common:
        copy.wait()
    before = jnp.max(flag[...].astype(F32)).astype(jnp.int32)
    pushed[0] = before
    patches = jnp.where(light, jnp.where(before > 1, 2, 1), 0)

    def cross(p, carry):
        for q in range(2):
            @pl.when(p == q)
            def _():
                for copy in copies[q]:
                    copy.wait()

        @pl.when(p < patches)
        def _():
            there = pl.multiple_of(half * (1 - p), half)
            own = own_2.at[p]
            nrm = nrm_2.at[p]
            normed, unit, inverse = norm_half(own[...], gain[...], own[:, pl.ds(first, 128)])
            nrm[pl.ds(there, half), :] = normed
            unit_o[p, :, pl.ds(there, half)] = unit
            inv_o[p, :, pl.ds(there, half)] = inverse
            patch_core(scal[0], p, nrm, dy_2.at[p], weights, wt, wo, send, keep, stats, wacc,
                       *work)

        return carry

    lax.fori_loop(0, 2, cross, 0)
    total = wacc[0:384] * factor
    gain_o[...] = jnp.sum(total * wt[...].astype(F32), axis=0, keepdims=True) / gain[...]
    for r in range(16):
        for c in range(4):
            block = wacc[32 * r:32 * r + 32, 128 * c:128 * c + 128]
            pieces[4 * r + c] = (block * factor).astype(BF16)


def pair_kernel(scal, keep, received, stats, stats_received, send, kept, stats_o):
    far = scal[3]
    send[...] = (keep[1 - far].astype(F32) + received[1 - far].astype(F32)).astype(BF16)
    kept[...] = (keep[far].astype(F32) + received[far].astype(F32)).astype(BF16)
    stats_o[...] = stats[...] + stats_received[...]


def branch_kernel(scal, kept, received, stats, stats_received, unit, stat, gain,
                  branch, back, ahead):
    half = branch.shape[2] // 2
    own_gain = gain[:, pl.ds(pl.multiple_of(scal[1] * 128, 128), 128)]
    own_gain = jnp.broadcast_to(own_gain, (128, 128)).T[:, 0:1]
    scaled = (kept[...].astype(F32) + received[...].astype(F32)) * own_gain
    mean = (stats[0:1, :] + stats_received[0:1, :]) * (1.0 / D)
    slope = (stats[1:2, :] + stats_received[1:2, :]) * (1.0 / D)
    rows = (stat[0, 0:1, :] * (scaled - mean - unit[0].astype(F32) * slope)).astype(BF16)
    branch[0] = rows

    @pl.when(pl.program_id(0) == 0)
    def _():
        ahead[...] = rows[:, half:]

    @pl.when(pl.program_id(0) == 1)
    def _():
        back[...] = rows[:, :half]


def total_kernel(scal, received, gain, gain_received, out):
    def add(i, total):
        return total + received[i].astype(F32)

    total = lax.fori_loop(0, received.shape[0], add, jnp.zeros(received.shape[1:], F32), unroll=8)
    low = total.astype(BF16)
    at = pl.ds(pl.multiple_of(scal[1] * 128, 128), 128)
    own_gain = jnp.broadcast_to(gain[:, at] + gain_received[:, at], (8, 128)).astype(BF16)

    def put(i, carry):
        out[i, 0:32, :] = low
        out[i, 32:40, :] = own_gain
        return carry

    lax.fori_loop(0, received.shape[0], put, 0, unroll=8)


def place_kernel(scal, order, before, cotangent, branch, from_before, from_after, out, placed):
    slot = pl.program_id(0)
    count = scal[2]
    patch = out.shape[1]
    half = patch // 2

    @pl.when(slot >= count)
    def _():
        out[...] = cotangent[...]

    @pl.when(slot < count)
    def _():
        local = before[0] > 1

        @pl.when(jnp.logical_and(slot == 0, jnp.logical_not(local)))
        def _():
            placed[:, 0:half] = from_before[...]

        @pl.when(jnp.logical_and(slot == 0, local))
        def _():
            placed[:, 0:half] = branch[1, :, half:]

        @pl.when(slot > 0)
        def _():
            placed[:, 0:half] = branch[jnp.maximum(slot - 1, 0), :, half:]

        @pl.when(slot < 2)
        def _():
            placed[:, half:] = branch[jnp.minimum(slot, 1), :, 0:half]

        @pl.when(slot == 2)
        def _():
            placed[:, half:] = from_after[...]

        places = order[pl.ds(slot, 1), :]
        rows = 256
        for r in range(patch // rows):
            index = lax.broadcasted_iota(jnp.int32, (rows, patch), 0) + rows * r
            chosen = (index == places).astype(BF16)
            moved = mm_nt(chosen, placed[...])
            own = cotangent[0, rows * r:rows * r + rows, :].astype(F32)
            out[0, rows * r:rows * r + rows, :] = (own + moved).astype(BF16)


def finish_kernel(received, qkv, out, gain):
    gain[...] = jnp.sum(received[:, 32:40, :].astype(F32), axis=0)[0:1]
    for t in range(3):
        for c in range(4):
            block = jnp.concatenate(
                [received[4 * (4 * t + r) + c, 0:32, :].astype(F32) for r in range(4)], axis=0
            )
            qkv[t, 128 * c:128 * c + 128, :] = block.T
    for r in range(4):
        for c in range(4):
            out[32 * r:32 * r + 32, 128 * c:128 * c + 128] = received[
                4 * (12 + r) + c, 0:32, :
            ].astype(F32)


def shards(points, order, counts, cotangent, norm_gain, w_qkv, w_out):
    slots, patch, width = points.shape
    half = patch // 2
    curve = lax.axis_size("curve")
    model_part = lax.axis_index("mp")
    core = model_part % 2
    far = model_part // 2
    scal = jnp.stack([core, model_part, counts[0], far]).astype(jnp.int32)
    gain_row = norm_gain.reshape(1, width)
    w3 = jnp.transpose(w_qkv, (1, 0, 2))
    sds = jax.ShapeDtypeStruct

    def passed(x, by):
        return lax.ppermute(x, "curve", [(i, (i + by) % curve) for i in range(curve)])

    def swapped(x, bit):
        return lax.ppermute(x, "mp", [(i, i ^ bit) for i in range(4)])

    pull, push = pl.pallas_call(
        halo_kernel,
        in_specs=[SMEM, ANY, ANY, ANY],
        out_specs=[VMEM] * 2,
        out_shape=[sds((2, half // 2, width), BF16), sds((2, half // 2 + 16, width), BF16)],
        scratch_shapes=[
            pltpu.VMEM((slots, patch), jnp.int32),
            pltpu.VMEM((4, patch, width), BF16),
            pltpu.SemaphoreType.DMA((5,)),
        ],
        compiler_params=params(60),
        name="halo",
    )(counts, order, points, cotangent)
    pull, push = passed(pull, -1), passed(push, 1)

    rows = [
        pltpu.VMEM((patch, width), BF16),
        pltpu.VMEM((patch, width), BF16),
        pltpu.VMEM((half, width), BF16),
    ]
    rows_2 = [
        pltpu.VMEM((16, width), BF16),
        pltpu.VMEM((2, patch, width), BF16),
        pltpu.VMEM((2, patch, width), BF16),
        pltpu.VMEM((2, half, width), BF16),
        pltpu.VMEM((width + 16, 384), BF16),
        pltpu.VMEM((384, width), BF16),
        pltpu.VMEM((128, width), BF16),
        pltpu.SemaphoreType.DMA((3, 7)),
    ]
    work = [
        pltpu.VMEM((384, patch), BF16),
        pltpu.VMEM((patch, 128), BF16),
        pltpu.VMEM((patch, 128), BF16),
        pltpu.VMEM((128, patch), BF16),
        pltpu.VMEM((128, patch), BF16),
        pltpu.VMEM((384, patch), BF16),
        pltpu.VMEM((width, patch), BF16),
        pltpu.VMEM((2, patch, patch), F32),
        pltpu.VMEM((2, patch, patch), BF16),
        pltpu.SemaphoreType.DMA((4,)),
    ]
    lanes = 2 * patch
    shared = [
        sds((2, 128, lanes), BF16),
        sds((2, 128, lanes), BF16),
        sds((2, lanes), F32),
        sds((2, 128, patch), BF16),
        sds((2, 8, patch), F32),
    ]
    send, keep, stats, unit, inverse, wacc, weights, wt, nrm, dy = pl.pallas_call(
        local_kernel,
        in_specs=[SMEM] + [VMEM] * 6,
        out_specs=[ANY] * 2 + [VMEM] * 8,
        out_shape=shared + [
            sds((512, width), F32),
            sds((width + 16, 384), BF16),
            sds((384, width), BF16),
            sds((2, half, width), BF16),
            sds((2, half, width), BF16),
        ],
        scratch_shapes=rows + work,
        compiler_params=params(60),
        cost_estimate=cost(16 * 10**9, 16 * 10**6),
        name="local",
    )(scal, order, points, cotangent, gain_row, w3, w_out)
    pull, push, wacc = lax.optimization_barrier((pull, push, wacc))

    factor = 1.0 / math.sqrt(curve * slots * patch)
    send, keep, stats, unit, inverse, pieces, gain_part, before = pl.pallas_call(
        functools.partial(cross_kernel, factor),
        in_specs=[SMEM] + [ANY] * 4 + [HBM] * 11 + [VMEM],
        out_specs=[ANY] * 2 + [VMEM] * 5 + [SMEM],
        out_shape=shared + [
            sds((64, 32, 128), BF16), sds((1, width), F32), sds((1,), jnp.int32)
        ],
        scratch_shapes=rows_2 + work + [pltpu.VMEM((512, width), F32)],
        input_output_aliases={5: 0, 6: 1},
        compiler_params=params(60),
        cost_estimate=cost(4 * 10**9, 8 * 10**6),
        name="cross",
    )(scal, pull, swapped(pull, 1), push, swapped(push, 1), send, keep, wacc, nrm, dy, stats, unit,
      inverse, weights, wt, w_out, gain_row)

    received = lax.all_to_all(pieces, "curve", 0, 0)
    gain_part = gain_part + swapped(gain_part, 1)
    gain_far = swapped(gain_part, 2)

    def whole(*shape):
        return pl.BlockSpec(shape, lambda i: (0,) * len(shape))

    def by_patch(*shape):
        return pl.BlockSpec((1,) + shape, lambda i: (i,) + (0,) * len(shape))

    def by_lanes(*shape):
        return pl.BlockSpec(shape + (patch,), lambda i: (0,) * len(shape) + (i,))

    near, near_stats = swapped(send, 1), swapped(stats, 1)
    send, kept, stats = pl.pallas_call(
        pair_kernel,
        grid=(2,),
        in_specs=[SMEM, by_lanes(2, 128), by_lanes(2, 128), by_lanes(2), by_lanes(2)],
        out_specs=[by_lanes(128), by_lanes(128), by_lanes(2)],
        out_shape=[sds((128, lanes), BF16), sds((128, lanes), BF16), sds((2, lanes), F32)],
        compiler_params=params(16),
        cost_estimate=cost(1000, 1000),
        name="pair",
    )(scal, keep, near, stats, near_stats)
    send, gain_far = lax.optimization_barrier((send, gain_far))
    away, away_stats = swapped(send, 2), swapped(stats, 2)
    branch, back, ahead = pl.pallas_call(
        branch_kernel,
        grid=(2,),
        in_specs=[SMEM, by_lanes(128), by_lanes(128), by_lanes(2), by_lanes(2),
                  by_patch(128, patch), by_patch(8, patch), whole(1, width)],
        out_specs=[by_patch(128, patch), whole(128, half), whole(128, half)],
        out_shape=[sds((2, 128, patch), BF16), sds((128, half), BF16), sds((128, half), BF16)],
        compiler_params=params(16),
        cost_estimate=cost(10**10, 1000),
        name="branch",
    )(scal, kept, away, stats, away_stats, unit, inverse, gain_row)
    from_before, from_after = passed(ahead, 1), passed(back, -1)

    totals = pl.pallas_call(
        total_kernel,
        in_specs=[SMEM] + [VMEM] * 3,
        out_specs=VMEM,
        out_shape=sds((64, 40, 128), BF16),
        compiler_params=params(16),
        name="total",
    )(scal, received, gain_part, gain_far)
    gathered = lax.all_to_all(totals, "curve", 0, 0)

    grad_points = pl.pallas_call(
        place_kernel,
        grid_spec=pltpu.PrefetchScalarGridSpec(
            num_scalar_prefetch=1,
            grid=(slots,),
            in_specs=[
                pl.BlockSpec((slots, patch), lambda i, s: (0, 0)),
                SMEM,
                pl.BlockSpec((1, patch, 128), lambda i, s: (i, 0, s[1])),
                pl.BlockSpec((2, 128, patch), lambda i, s: (0, 0, 0)),
                pl.BlockSpec((128, half), lambda i, s: (0, 0)),
                pl.BlockSpec((128, half), lambda i, s: (0, 0)),
            ],
            out_specs=pl.BlockSpec((1, patch, 128), lambda i, s: (i, 0, 0)),
            scratch_shapes=[pltpu.VMEM((128, patch), BF16)],
        ),
        out_shape=sds((slots, patch, 128), BF16),
        compiler_params=params(16),
        cost_estimate=cost(10**10, 1000),
        name="place",
    )(scal, order, before, cotangent, branch, from_before, from_after)

    grad_qkv, grad_out, grad_gain = pl.pallas_call(
        finish_kernel,
        in_specs=[VMEM],
        out_specs=[VMEM] * 3,
        out_shape=[sds((3, width, 128), F32), sds((128, width), F32), sds((1, 128), F32)],
        compiler_params=params(16),
        name="finish",
    )(gathered)
    return grad_points, grad_gain.reshape(128), jnp.transpose(grad_qkv, (1, 0, 2)), grad_out


def solution(mesh):
    in_specs = (
        P("curve", None, None),
        P("curve", None),
        P("curve"),
        P("curve", None, None),
        P(),
        P(None, None, "mp"),
        P("mp", None),
    )
    out_specs = (P("curve", None, "mp"), P("mp"), P(None, None, "mp"), P("mp", None))
    return jax.shard_map(shards, mesh=mesh, in_specs=in_specs, out_specs=out_specs, check_vma=False)
```

```python
import functools
import math

import jax
import jax.numpy as jnp
from jax import lax
from jax.experimental import pallas as pl
from jax.experimental.pallas import tpu as pltpu
from jax.sharding import PartitionSpec as P

D = 512
HEADS = 8
HEAD = D // HEADS
EPSILON = 1e-05
SCALE = HEAD ** (-0.5) * math.log2(math.e)

F32 = jnp.float32
BF16 = jnp.bfloat16
NT = (((1,), (1,)), ((), ()))
VMEM = pl.BlockSpec(memory_space=pltpu.VMEM)
SMEM = pl.BlockSpec(memory_space=pltpu.SMEM)
ANY = pl.BlockSpec(memory_space=pl.ANY)
HBM = pl.BlockSpec(memory_space=pltpu.HBM)


def mm(a, b):
    return jnp.dot(a, b, preferred_element_type=F32)


def mm_nt(a, b):
    return lax.dot_general(a, b, NT, preferred_element_type=F32)


def params(mib):
    return pltpu.CompilerParams(vmem_limit_bytes=mib * 1024 * 1024)


def cost(flops, bytes_accessed):
    return pl.CostEstimate(flops=flops, bytes_accessed=bytes_accessed, transcendentals=0)


def one_hot_rows(places, patch):
    count = places.shape[1]
    column = jnp.broadcast_to(places, (128, count)).T
    lanes = lax.broadcasted_iota(jnp.int32, (count, 128), 1)
    return jnp.concatenate(
        [(column == lanes + 128 * b).astype(BF16) for b in range(patch // 128)], axis=1
    )


def halo_kernel(counts, order_i, points, cotangent, pull, push, order, held, done):
    rows = pull.shape[1]
    patch = points.shape[1]
    last = points.shape[0] - 1
    core = lax.axis_index("mp") % 2
    places = pltpu.make_async_copy(order_i, order, done.at[4])
    places.start()
    copies = []
    for slot in (last, 0):
        for source in (points, cotangent):
            k = len(copies)
            copies.append(pltpu.make_async_copy(source.at[slot], held.at[k], done.at[k]))
            copies[-1].start()
    count = jnp.zeros((16, push.shape[2]), F32) + counts[0].astype(F32)
    push[0, rows:, :] = count.astype(BF16)
    push[1, rows:, :] = count.astype(BF16)
    places.wait()
    for k, (slot, base, out) in enumerate(((last, patch // 2, push), (0, 0, pull))):
        at = pl.ds(pl.multiple_of(base + core * rows, rows), rows)
        chosen = one_hot_rows(order[slot:slot + 1, at], patch)
        for j in range(2):
            copies[2 * k + j].wait()
            out[j, 0:rows, :] = mm(chosen, held[2 * k + j]).astype(BF16)


def norm_half(x, gain, own):
    values = x.astype(F32)
    mean = jnp.mean(values, axis=1, keepdims=True)
    centre = values - mean
    inverse = lax.rsqrt(jnp.mean(centre * centre, axis=1, keepdims=True) + EPSILON)
    normed = (centre * inverse * gain).astype(BF16)
    unit = ((own.astype(F32) - mean) * inverse).T.astype(BF16)
    inverse_row = jnp.broadcast_to(inverse, (x.shape[0], 128)).T[0:8]
    return normed, unit, inverse_row


def project(nrm, dy, weights, wt, wo, prj, kr, vr, dat):
    prj[0:128, :] = (mm_nt(wt[0:128, :], nrm[...]) * SCALE).astype(BF16)
    prj[128:384, :] = mm_nt(wt[128:384, :], nrm[...]).astype(BF16)
    both = mm(nrm[...], weights[0:D, 128:384]).astype(BF16)
    kr[...] = both[:, 0:128]
    vr[...] = both[:, 128:256]
    dat[...] = mm_nt(wo[...], dy[...]).astype(BF16)


def attend(prj, kr, vr, dat, gp, att, scores, lows):
    patch = prj.shape[1]
    chunk = 256
    blocks = [slice(c, c + chunk) for c in range(0, patch, chunk)]
    zeros = jnp.zeros((HEAD, patch), BF16)
    state = [{}, {}]

    def pad(x, h):
        return jnp.concatenate([x, zeros] if h == 0 else [zeros, x], axis=0)

    def fold(x, op):
        return op(x.reshape(chunk // 8, 8, patch), axis=0)

    def score(h, keys):
        here, lo = state[h], h * HEAD
        block = mm(kr[keys, :], pad(prj[lo:lo + HEAD, :], h))
        scores[h, keys, :] = block
        high = fold(block, jnp.max)
        here["high"] = jnp.maximum(here["high"], high) if "high" in here else high
        if keys.stop == patch:
            here["high"] = jnp.max(here["high"], axis=0, keepdims=True)

    def soften(h, keys):
        here, lo = state[h], h * HEAD
        expos = jnp.exp2(scores[h, keys, :] - here["high"])
        scores[h, keys, :] = expos
        lows[h, keys, :] = expos.astype(BF16)
        total = fold(expos, jnp.sum)
        here["total"] = here["total"] + total if "total" in here else total
        if keys.stop == patch:
            recip = 1.0 / jnp.sum(here["total"], axis=0, keepdims=True)
            attended = mm(prj[256 + lo:256 + lo + HEAD, :], lows[h]) * recip
            att[lo:lo + HEAD, :] = attended.astype(BF16)
            grad = dat[lo:lo + HEAD, :].astype(F32) * recip
            here["inner"] = jnp.sum(grad * attended, axis=0, keepdims=True)
            here["grad"] = grad.astype(BF16)

    def back(h, keys):
        here, lo = state[h], h * HEAD
        grad_probs = mm(vr[keys, :], pad(here["grad"], h))
        grad_scores = (scores[h, keys, :] * (grad_probs - here["inner"])).astype(BF16)
        dk = mm_nt(prj[lo:lo + HEAD, :], grad_scores) * (HEAD ** (-0.5) / SCALE)
        gp[128 + lo:128 + lo + HEAD, keys] = dk.astype(BF16)
        gp[256 + lo:256 + lo + HEAD, keys] = mm_nt(here["grad"], lows[h, keys, :]).astype(BF16)
        lows[h, keys, :] = grad_scores
        if keys.stop == patch:
            dq = mm(prj[128 + lo:128 + lo + HEAD, :], lows[h]) * (HEAD ** (-0.5))
            gp[lo:lo + HEAD, :] = dq.astype(BF16)

    for keys in blocks:
        score(0, keys)
    for keys in blocks:
        score(1, keys)
        soften(0, keys)
    for keys in blocks:
        back(0, keys)
        soften(1, keys)
    for keys in blocks:
        back(1, keys)


def split3(x):
    first = x.astype(BF16)
    rest = x - first.astype(F32)
    second = rest.astype(BF16)
    third = (rest - second.astype(F32)).astype(BF16)
    none = jnp.zeros((13, x.shape[1]), BF16)
    return jnp.concatenate([first, second, third, none], axis=0)


def load_weights(w3, wt, gain, weights):
    for t in range(3):
        weights[0:D, 128 * t:128 * t + 128] = w3[t]
    sums = jnp.sum(mm_nt(split3(gain[...]), wt[...]), axis=0, keepdims=True)
    weights[D:D + 16, :] = split3(sums)


def block_copies(core, p, send, keep, grads, done):
    patch = grads.shape[2]
    cols = pl.ds(pl.multiple_of(p * patch, patch), patch)
    copies = []
    for j in range(2):
        for k, (block, into) in enumerate(((2 * j + 1 - core, send), (2 * j + core, keep))):
            rows = pl.ds(pl.multiple_of(block * 128, 128), 128)
            copies.append(pltpu.make_async_copy(
                grads.at[p, rows], into.at[j, :, cols], done.at[p, 2 * j + k]
            ))
    return copies


def patch_core(core, p, nrm, dy, weights, wt, wo, send, keep, stats, wacc,
               prj, kr, vr, dat, att, gp, grads, scores, lows, done):
    project(nrm, dy, weights, wt, wo, prj, kr, vr, dat)
    attend(prj, kr, vr, dat, gp, att, scores, lows)
    patch = gp.shape[1]
    cols = pl.ds(pl.multiple_of(p * patch, patch), patch)
    grads[p] = mm(weights[0:D, :], gp[...]).astype(BF16)
    for copy in block_copies(core, p, send, keep, grads, done):
        copy.start()
    wacc[0:384] += mm(gp[...], nrm[...])
    wacc[384:512] += mm(att[...], dy[...])
    stats[0:1, cols] = jnp.sum(mm(weights[D:D + 16, :], gp[...]), axis=0, keepdims=True)
    stats[1:2, cols] = second_stat(gp, prj)


def second_stat(gp, prj):
    product = gp[...].astype(F32) * prj[...].astype(F32)
    queries = jnp.sum(product[0:128], axis=0, keepdims=True) * (1.0 / SCALE)
    return queries + jnp.sum(product[128:384], axis=0, keepdims=True)


def gather_rows(scal, order, points, cotangent, gain, own, slot, side, into_x, into_dy):
    patch = points.shape[1]
    half = patch // 2
    first = pl.multiple_of(scal[1] * 128, 128)
    chosen = one_hot_rows(order[pl.ds(slot, 1), half * side:half * side + half], patch)
    x = mm(chosen, points[slot]).astype(BF16)
    into_dy[...] = mm(chosen, cotangent[slot]).astype(BF16)
    own[...] = x
    normed, unit, inverse = norm_half(x, gain[...], own[:, pl.ds(first, 128)])
    into_x[...] = normed
    return unit, inverse


def local_kernel(scal, order, points, cotangent, gain, w3, wo,
                 send, keep, stats, unit_o, inv_o, wacc, weights, wt, nrm_o, dy_o,
                 nrm, dy, own, *work):
    half = points.shape[1] // 2
    for t in range(3):
        wt[128 * t:128 * t + 128, :] = w3[t].astype(F32).T.astype(BF16)
    wacc[...] = jnp.zeros_like(wacc)
    load_weights(w3, wt, gain, weights)

    whole = scal[2] > 1

    def step(p, carry):
        for side in range(2):
            rows = slice(half * side, half * side + half)

            @pl.when(jnp.logical_or(whole, p == side))
            def _():
                slot = jnp.where(whole, p + side, 0)
                unit, inverse = gather_rows(scal, order, points, cotangent, gain, own, slot,
                                            1 - side, nrm.at[rows], dy.at[rows])
                unit_o[p, :, rows] = unit
                inv_o[p, :, rows] = inverse

        @pl.when(whole)
        def _():
            patch_core(scal[0], p, nrm, dy, weights, wt, wo, send, keep, stats, wacc, *work)

        @pl.when(jnp.logical_not(whole))
        def _():
            here = pl.ds(pl.multiple_of(half * p, half), half)
            nrm_o[p] = nrm[here, :]
            dy_o[p] = dy[here, :]

        return carry

    lax.fori_loop(0, 2, step, 0)

    @pl.when(whole)
    def _():
        for p in range(2):
            for copy in block_copies(scal[0], p, send, keep, work[-4], work[-1]):
                copy.wait()


def cross_kernel(factor, scal, pull, pull_other, push, push_other, send_i, keep_i, wacc_i, nrm_i,
                 dy_i, stats_i, unit_i, inv_i, weights_i, wt_i, wo_i, gain,
                 send, keep, stats, unit_o, inv_o, pieces, gain_o, pushed,
                 flag, nrm_2, dy_2, own_2, weights, wt, wo, arrived, *work_wacc):
    wacc, work = work_wacc[-1], work_wacc[:-1]
    half = nrm_i.shape[1]
    part = half // 2
    first = pl.multiple_of(scal[1] * 128, 128)
    light = scal[2] == 1
    told = pltpu.make_async_copy(push.at[0, part:part + 16], flag, arrived.at[2, 0])
    told.start()
    copies = []
    common = ((stats_i, stats), (unit_i, unit_o), (inv_i, inv_o), (weights_i, weights), (wt_i, wt),
              (wo_i, wo))
    common = [pltpu.make_async_copy(source, into, arrived.at[2, k + 1])
              for k, (source, into) in enumerate(common)]
    for p, one, other in ((0, pull, pull_other), (1, push, push_other)):
        here, there = half * p, half * (1 - p)
        moves = [(nrm_i.at[p], nrm_2.at[p, here:here + half]),
                 (dy_i.at[p], dy_2.at[p, here:here + half])]
        for source, core in ((one, scal[0]), (other, 1 - scal[0])):
            at = pl.multiple_of(core * part, part)
            moves.append((source.at[0, 0:part], own_2.at[p, pl.ds(at, part)]))
            moves.append((source.at[1, 0:part],
                          dy_2.at[p, pl.ds(pl.multiple_of(there + at, part), part)]))
        copies.append([pltpu.make_async_copy(source, into, arrived.at[p, k])
                       for k, (source, into) in enumerate(moves)])
        for copy in copies[-1]:
            copy.start()
        if p == 0:
            for copy in common:
                copy.start()
    @pl.when(light)
    def _():
        wacc[...] = jnp.zeros_like(wacc)

    @pl.when(jnp.logical_not(light))
    def _():
        copy = pltpu.make_async_copy(wacc_i, wacc, arrived.at[3, 0])
        copy.start()
        copy.wait()

    told.wait()
    for copy in common:
        copy.wait()
    before = jnp.max(flag[...].astype(F32)).astype(jnp.int32)
    pushed[0] = before
    patches = jnp.where(light, jnp.where(before > 1, 2, 1), 0)

    def cross(p, carry):
        for q in range(2):
            @pl.when(p == q)
            def _():
                for copy in copies[q]:
                    copy.wait()

        @pl.when(p < patches)
        def _():
            there = pl.multiple_of(half * (1 - p), half)
            own = own_2.at[p]
            nrm = nrm_2.at[p]
            normed, unit, inverse = norm_half(own[...], gain[...], own[:, pl.ds(first, 128)])
            nrm[pl.ds(there, half), :] = normed
            unit_o[p, :, pl.ds(there, half)] = unit
            inv_o[p, :, pl.ds(there, half)] = inverse
            patch_core(scal[0], p, nrm, dy_2.at[p], weights, wt, wo, send, keep, stats, wacc,
                       *work)

        return carry

    lax.fori_loop(0, 2, cross, 0)
    total = wacc[0:384] * factor
    gain_o[...] = jnp.sum(total * wt[...].astype(F32), axis=0, keepdims=True) / gain[...]
    for r in range(16):
        for c in range(4):
            block = wacc[32 * r:32 * r + 32, 128 * c:128 * c + 128]
            pieces[4 * r + c] = (block * factor).astype(BF16)
    for p in range(2):
        @pl.when(p < patches)
        def _():
            for copy in block_copies(scal[0], p, send, keep, work[-4], work[-1]):
                copy.wait()


def pair_kernel(scal, keep, received, stats, stats_received, send, kept, stats_o):
    far = scal[3]
    send[...] = (keep[1 - far].astype(F32) + received[1 - far].astype(F32)).astype(BF16)
    kept[...] = (keep[far].astype(F32) + received[far].astype(F32)).astype(BF16)
    stats_o[...] = stats[...] + stats_received[...]


def branch_kernel(scal, kept, received, stats, stats_received, unit, stat, gain,
                  branch, back, ahead):
    half = branch.shape[2] // 2
    own_gain = gain[:, pl.ds(pl.multiple_of(scal[1] * 128, 128), 128)]
    own_gain = jnp.broadcast_to(own_gain, (128, 128)).T[:, 0:1]
    scaled = (kept[...].astype(F32) + received[...].astype(F32)) * own_gain
    mean = (stats[0:1, :] + stats_received[0:1, :]) * (1.0 / D)
    slope = (stats[1:2, :] + stats_received[1:2, :]) * (1.0 / D)
    rows = (stat[0, 0:1, :] * (scaled - mean - unit[0].astype(F32) * slope)).astype(BF16)
    branch[0] = rows

    @pl.when(pl.program_id(0) == 0)
    def _():
        ahead[...] = rows[:, half:]

    @pl.when(pl.program_id(0) == 1)
    def _():
        back[...] = rows[:, :half]


def total_kernel(scal, received, gain, gain_received, out):
    def add(i, total):
        return total + received[i].astype(F32)

    total = lax.fori_loop(0, received.shape[0], add, jnp.zeros(received.shape[1:], F32), unroll=8)
    low = total.astype(BF16)
    at = pl.ds(pl.multiple_of(scal[1] * 128, 128), 128)
    own_gain = jnp.broadcast_to(gain[:, at] + gain_received[:, at], (8, 128)).astype(BF16)

    def put(i, carry):
        out[i, 0:32, :] = low
        out[i, 32:40, :] = own_gain
        return carry

    lax.fori_loop(0, received.shape[0], put, 0, unroll=8)


def place_kernel(scal, order, before, cotangent, branch, from_before, from_after, out, placed):
    slot = pl.program_id(0)
    count = scal[2]
    patch = out.shape[1]
    half = patch // 2

    @pl.when(slot >= count)
    def _():
        out[...] = cotangent[...]

    @pl.when(slot < count)
    def _():
        local = before[0] > 1

        @pl.when(jnp.logical_and(slot == 0, jnp.logical_not(local)))
        def _():
            placed[:, 0:half] = from_before[...]

        @pl.when(jnp.logical_and(slot == 0, local))
        def _():
            placed[:, 0:half] = branch[1, :, half:]

        @pl.when(slot > 0)
        def _():
            placed[:, 0:half] = branch[jnp.maximum(slot - 1, 0), :, half:]

        @pl.when(slot < 2)
        def _():
            placed[:, half:] = branch[jnp.minimum(slot, 1), :, 0:half]

        @pl.when(slot == 2)
        def _():
            placed[:, half:] = from_after[...]

        places = order[pl.ds(slot, 1), :]
        rows = 256
        for r in range(patch // rows):
            index = lax.broadcasted_iota(jnp.int32, (rows, patch), 0) + rows * r
            chosen = (index == places).astype(BF16)
            moved = mm_nt(chosen, placed[...])
            own = cotangent[0, rows * r:rows * r + rows, :].astype(F32)
            out[0, rows * r:rows * r + rows, :] = (own + moved).astype(BF16)


def finish_kernel(received, qkv, out, gain):
    gain[...] = jnp.sum(received[:, 32:40, :].astype(F32), axis=0)[0:1]
    for t in range(3):
        for c in range(4):
            block = jnp.concatenate(
                [received[4 * (4 * t + r) + c, 0:32, :].astype(F32) for r in range(4)], axis=0
            )
            qkv[t, 128 * c:128 * c + 128, :] = block.T
    for r in range(4):
        for c in range(4):
            out[32 * r:32 * r + 32, 128 * c:128 * c + 128] = received[
                4 * (12 + r) + c, 0:32, :
            ].astype(F32)


def shards(points, order, counts, cotangent, norm_gain, w_qkv, w_out):
    slots, patch, width = points.shape
    half = patch // 2
    curve = lax.axis_size("curve")
    model_part = lax.axis_index("mp")
    core = model_part % 2
    far = model_part // 2
    scal = jnp.stack([core, model_part, counts[0], far]).astype(jnp.int32)
    gain_row = norm_gain.reshape(1, width)
    w3 = jnp.transpose(w_qkv, (1, 0, 2))
    sds = jax.ShapeDtypeStruct

    def passed(x, by):
        return lax.ppermute(x, "curve", [(i, (i + by) % curve) for i in range(curve)])

    def swapped(x, bit):
        return lax.ppermute(x, "mp", [(i, i ^ bit) for i in range(4)])

    pull, push = pl.pallas_call(
        halo_kernel,
        in_specs=[SMEM, ANY, ANY, ANY],
        out_specs=[VMEM] * 2,
        out_shape=[sds((2, half // 2, width), BF16), sds((2, half // 2 + 16, width), BF16)],
        scratch_shapes=[
            pltpu.VMEM((slots, patch), jnp.int32),
            pltpu.VMEM((4, patch, width), BF16),
            pltpu.SemaphoreType.DMA((5,)),
        ],
        compiler_params=params(60),
        name="halo",
    )(counts, order, points, cotangent)
    pull, push = passed(pull, -1), passed(push, 1)

    rows = [
        pltpu.VMEM((patch, width), BF16),
        pltpu.VMEM((patch, width), BF16),
        pltpu.VMEM((half, width), BF16),
    ]
    rows_2 = [
        pltpu.VMEM((16, width), BF16),
        pltpu.VMEM((2, patch, width), BF16),
        pltpu.VMEM((2, patch, width), BF16),
        pltpu.VMEM((2, half, width), BF16),
        pltpu.VMEM((width + 16, 384), BF16),
        pltpu.VMEM((384, width), BF16),
        pltpu.VMEM((128, width), BF16),
        pltpu.SemaphoreType.DMA((4, 7)),
    ]
    work = [
        pltpu.VMEM((384, patch), BF16),
        pltpu.VMEM((patch, 128), BF16),
        pltpu.VMEM((patch, 128), BF16),
        pltpu.VMEM((128, patch), BF16),
        pltpu.VMEM((128, patch), BF16),
        pltpu.VMEM((384, patch), BF16),
        pltpu.VMEM((2, width, patch), BF16),
        pltpu.VMEM((2, patch, patch), F32),
        pltpu.VMEM((2, patch, patch), BF16),
        pltpu.SemaphoreType.DMA((2, 4)),
    ]
    lanes = 2 * patch
    shared = [
        sds((2, 128, lanes), BF16),
        sds((2, 128, lanes), BF16),
        sds((2, lanes), F32),
        sds((2, 128, patch), BF16),
        sds((2, 8, patch), F32),
    ]
    send, keep, stats, unit, inverse, wacc, weights, wt, nrm, dy = pl.pallas_call(
        local_kernel,
        in_specs=[SMEM] + [VMEM] * 6,
        out_specs=[ANY] * 2 + [VMEM] * 8,
        out_shape=shared + [
            sds((512, width), F32),
            sds((width + 16, 384), BF16),
            sds((384, width), BF16),
            sds((2, half, width), BF16),
            sds((2, half, width), BF16),
        ],
        scratch_shapes=rows + work,
        compiler_params=params(60),
        cost_estimate=cost(16 * 10**9, 16 * 10**6),
        name="local",
    )(scal, order, points, cotangent, gain_row, w3, w_out)
    pull, push, wacc = lax.optimization_barrier((pull, push, wacc))

    factor = 1.0 / math.sqrt(curve * slots * patch)
    send, keep, stats, unit, inverse, pieces, gain_part, before = pl.pallas_call(
        functools.partial(cross_kernel, factor),
        in_specs=[SMEM] + [HBM] * 15 + [VMEM],
        out_specs=[ANY] * 2 + [VMEM] * 5 + [SMEM],
        out_shape=shared + [
            sds((64, 32, 128), BF16), sds((1, width), F32), sds((1,), jnp.int32)
        ],
        scratch_shapes=rows_2 + work + [pltpu.VMEM((512, width), F32)],
        input_output_aliases={5: 0, 6: 1},
        compiler_params=params(60),
        cost_estimate=cost(4 * 10**9, 8 * 10**6),
        name="cross",
    )(scal, pull, swapped(pull, 1), push, swapped(push, 1), send, keep, wacc, nrm, dy, stats, unit,
      inverse, weights, wt, w_out, gain_row)

    received = lax.all_to_all(pieces, "curve", 0, 0)
    gain_part = gain_part + swapped(gain_part, 1)
    gain_far = swapped(gain_part, 2)

    def whole(*shape):
        return pl.BlockSpec(shape, lambda i: (0,) * len(shape))

    def by_patch(*shape):
        return pl.BlockSpec((1,) + shape, lambda i: (i,) + (0,) * len(shape))

    def by_lanes(*shape):
        return pl.BlockSpec(shape + (patch,), lambda i: (0,) * len(shape) + (i,))

    near, near_stats = swapped(send, 1), swapped(stats, 1)
    send, kept, stats = pl.pallas_call(
        pair_kernel,
        grid=(2,),
        in_specs=[SMEM, by_lanes(2, 128), by_lanes(2, 128), by_lanes(2), by_lanes(2)],
        out_specs=[by_lanes(128), by_lanes(128), by_lanes(2)],
        out_shape=[sds((128, lanes), BF16), sds((128, lanes), BF16), sds((2, lanes), F32)],
        compiler_params=params(16),
        cost_estimate=cost(1000, 1000),
        name="pair",
    )(scal, keep, near, stats, near_stats)
    send, gain_far = lax.optimization_barrier((send, gain_far))
    away, away_stats = swapped(send, 2), swapped(stats, 2)
    branch, back, ahead = pl.pallas_call(
        branch_kernel,
        grid=(2,),
        in_specs=[SMEM, by_lanes(128), by_lanes(128), by_lanes(2), by_lanes(2),
                  by_patch(128, patch), by_patch(8, patch), whole(1, width)],
        out_specs=[by_patch(128, patch), whole(128, half), whole(128, half)],
        out_shape=[sds((2, 128, patch), BF16), sds((128, half), BF16), sds((128, half), BF16)],
        compiler_params=params(16),
        cost_estimate=cost(10**10, 1000),
        name="branch",
    )(scal, kept, away, stats, away_stats, unit, inverse, gain_row)
    from_before, from_after = passed(ahead, 1), passed(back, -1)

    totals = pl.pallas_call(
        total_kernel,
        in_specs=[SMEM] + [VMEM] * 3,
        out_specs=VMEM,
        out_shape=sds((64, 40, 128), BF16),
        compiler_params=params(16),
        name="total",
    )(scal, received, gain_part, gain_far)
    gathered = lax.all_to_all(totals, "curve", 0, 0)

    grad_points = pl.pallas_call(
        place_kernel,
        grid_spec=pltpu.PrefetchScalarGridSpec(
            num_scalar_prefetch=1,
            grid=(slots,),
            in_specs=[
                pl.BlockSpec((slots, patch), lambda i, s: (0, 0)),
                SMEM,
                pl.BlockSpec((1, patch, 128), lambda i, s: (i, 0, s[1])),
                pl.BlockSpec((2, 128, patch), lambda i, s: (0, 0, 0)),
                pl.BlockSpec((128, half), lambda i, s: (0, 0)),
                pl.BlockSpec((128, half), lambda i, s: (0, 0)),
            ],
            out_specs=pl.BlockSpec((1, patch, 128), lambda i, s: (i, 0, 0)),
            scratch_shapes=[pltpu.VMEM((128, patch), BF16)],
        ),
        out_shape=sds((slots, patch, 128), BF16),
        compiler_params=params(16),
        cost_estimate=cost(10**10, 1000),
        name="place",
    )(scal, order, before, cotangent, branch, from_before, from_after)

    grad_qkv, grad_out, grad_gain = pl.pallas_call(
        finish_kernel,
        in_specs=[VMEM],
        out_specs=[VMEM] * 3,
        out_shape=[sds((3, width, 128), F32), sds((128, width), F32), sds((1, 128), F32)],
        compiler_params=params(16),
        name="finish",
    )(gathered)
    return grad_points, grad_gain.reshape(128), jnp.transpose(grad_qkv, (1, 0, 2)), grad_out


def solution(mesh):
    in_specs = (
        P("curve", None, None),
        P("curve", None),
        P("curve"),
        P("curve", None, None),
        P(),
        P(None, None, "mp"),
        P("mp", None),
    )
    out_specs = (P("curve", None, "mp"), P("mp"), P(None, None, "mp"), P("mp", None))
    return jax.shard_map(shards, mesh=mesh, in_specs=in_specs, out_specs=out_specs, check_vma=False)
```

```python
import functools
import math

import jax
import jax.numpy as jnp
from jax import lax
from jax.experimental import pallas as pl
from jax.experimental.pallas import tpu as pltpu
from jax.sharding import PartitionSpec as P

D = 512
HEADS = 8
HEAD = D // HEADS
EPSILON = 1e-05
SCALE = HEAD ** (-0.5) * math.log2(math.e)

F32 = jnp.float32
BF16 = jnp.bfloat16
NT = (((1,), (1,)), ((), ()))
VMEM = pl.BlockSpec(memory_space=pltpu.VMEM)
SMEM = pl.BlockSpec(memory_space=pltpu.SMEM)
ANY = pl.BlockSpec(memory_space=pl.ANY)
HBM = pl.BlockSpec(memory_space=pltpu.HBM)


def mm(a, b):
    return jnp.dot(a, b, preferred_element_type=F32)


def mm_nt(a, b):
    return lax.dot_general(a, b, NT, preferred_element_type=F32)


def params(mib):
    return pltpu.CompilerParams(vmem_limit_bytes=mib * 1024 * 1024)


def cost(flops, bytes_accessed):
    return pl.CostEstimate(flops=flops, bytes_accessed=bytes_accessed, transcendentals=0)


def one_hot_rows(places, patch):
    count = places.shape[1]
    column = jnp.broadcast_to(places, (128, count)).T
    lanes = lax.broadcasted_iota(jnp.int32, (count, 128), 1)
    return jnp.concatenate(
        [(column == lanes + 128 * b).astype(BF16) for b in range(patch // 128)], axis=1
    )


def halo_kernel(counts, order_i, points, cotangent, pull, push, order, held, done):
    rows = pull.shape[1]
    patch = points.shape[1]
    last = points.shape[0] - 1
    core = lax.axis_index("mp") % 2
    places = pltpu.make_async_copy(order_i, order, done.at[4])
    places.start()
    copies = []
    for slot in (last, 0):
        for source in (points, cotangent):
            k = len(copies)
            copies.append(pltpu.make_async_copy(source.at[slot], held.at[k], done.at[k]))
            copies[-1].start()
    count = jnp.zeros((16, push.shape[2]), F32) + counts[0].astype(F32)
    push[0, rows:, :] = count.astype(BF16)
    push[1, rows:, :] = count.astype(BF16)
    places.wait()
    for k, (slot, base, out) in enumerate(((last, patch // 2, push), (0, 0, pull))):
        at = pl.ds(pl.multiple_of(base + core * rows, rows), rows)
        chosen = one_hot_rows(order[slot:slot + 1, at], patch)
        for j in range(2):
            copies[2 * k + j].wait()
            out[j, 0:rows, :] = mm(chosen, held[2 * k + j]).astype(BF16)


def norm_half(x, gain, own):
    values = x.astype(F32)
    mean = jnp.mean(values, axis=1, keepdims=True)
    centre = values - mean
    inverse = lax.rsqrt(jnp.mean(centre * centre, axis=1, keepdims=True) + EPSILON)
    normed = (centre * inverse * gain).astype(BF16)
    unit = ((own.astype(F32) - mean) * inverse).T.astype(BF16)
    inverse_row = jnp.broadcast_to(inverse, (x.shape[0], 128)).T[0:8]
    return normed, unit, inverse_row


def project(nrm, dy, weights, wt, wo, prj, kr, vr, dat):
    prj[0:128, :] = (mm_nt(wt[0:128, :], nrm[...]) * SCALE).astype(BF16)
    prj[128:384, :] = mm_nt(wt[128:384, :], nrm[...]).astype(BF16)
    both = mm(nrm[...], weights[0:D, 128:384]).astype(BF16)
    kr[...] = both[:, 0:128]
    vr[...] = both[:, 128:256]
    dat[...] = mm_nt(wo[...], dy[...]).astype(BF16)


def attend(prj, kr, vr, dat, gp, att, scores, lows):
    patch = prj.shape[1]
    chunk = 256
    blocks = [slice(c, c + chunk) for c in range(0, patch, chunk)]
    zeros = jnp.zeros((HEAD, patch), BF16)
    state = [{}, {}]

    def pad(x, h):
        return jnp.concatenate([x, zeros] if h == 0 else [zeros, x], axis=0)

    def fold(x, op):
        return op(x.reshape(chunk // 8, 8, patch), axis=0)

    def score(h, keys):
        here, lo = state[h], h * HEAD
        block = mm(kr[keys, :], pad(prj[lo:lo + HEAD, :], h))
        scores[h, keys, :] = block
        high = fold(block, jnp.max)
        here["high"] = jnp.maximum(here["high"], high) if "high" in here else high
        if keys.stop == patch:
            here["high"] = jnp.max(here["high"], axis=0, keepdims=True)

    def soften(h, keys):
        here, lo = state[h], h * HEAD
        expos = jnp.exp2(scores[h, keys, :] - here["high"])
        scores[h, keys, :] = expos
        lows[h, keys, :] = expos.astype(BF16)
        total = fold(expos, jnp.sum)
        here["total"] = here["total"] + total if "total" in here else total
        if keys.stop == patch:
            recip = 1.0 / jnp.sum(here["total"], axis=0, keepdims=True)
            attended = mm(prj[256 + lo:256 + lo + HEAD, :], lows[h]) * recip
            att[lo:lo + HEAD, :] = attended.astype(BF16)
            grad = dat[lo:lo + HEAD, :].astype(F32) * recip
            here["inner"] = jnp.sum(grad * attended, axis=0, keepdims=True)
            here["grad"] = grad.astype(BF16)

    def back(h, keys):
        here, lo = state[h], h * HEAD
        grad_probs = mm(vr[keys, :], pad(here["grad"], h))
        grad_scores = (scores[h, keys, :] * (grad_probs - here["inner"])).astype(BF16)
        dk = mm_nt(prj[lo:lo + HEAD, :], grad_scores) * (HEAD ** (-0.5) / SCALE)
        gp[128 + lo:128 + lo + HEAD, keys] = dk.astype(BF16)
        gp[256 + lo:256 + lo + HEAD, keys] = mm_nt(here["grad"], lows[h, keys, :]).astype(BF16)
        lows[h, keys, :] = grad_scores
        if keys.stop == patch:
            dq = mm(prj[128 + lo:128 + lo + HEAD, :], lows[h]) * (HEAD ** (-0.5))
            gp[lo:lo + HEAD, :] = dq.astype(BF16)

    for keys in blocks:
        score(0, keys)
    for keys in blocks:
        score(1, keys)
        soften(0, keys)
    for keys in blocks:
        back(0, keys)
        soften(1, keys)
    for keys in blocks:
        back(1, keys)


def split3(x):
    first = x.astype(BF16)
    rest = x - first.astype(F32)
    second = rest.astype(BF16)
    third = (rest - second.astype(F32)).astype(BF16)
    none = jnp.zeros((13, x.shape[1]), BF16)
    return jnp.concatenate([first, second, third, none], axis=0)


def load_weights(w3, wt, gain, weights):
    for t in range(3):
        weights[0:D, 128 * t:128 * t + 128] = w3[t]
    sums = jnp.sum(mm_nt(split3(gain[...]), wt[...]), axis=0, keepdims=True)
    weights[D:D + 16, :] = split3(sums)


def block_copies(core, p, send, keep, grads, done):
    patch = grads.shape[2]
    cols = pl.ds(pl.multiple_of(p * patch, patch), patch)
    copies = []
    for j in range(2):
        for k, (block, into) in enumerate(((2 * j + 1 - core, send), (2 * j + core, keep))):
            rows = pl.ds(pl.multiple_of(block * 128, 128), 128)
            copies.append(pltpu.make_async_copy(
                grads.at[p, rows], into.at[j, :, cols], done.at[p, 2 * j + k]
            ))
    return copies


def patch_core(core, p, nrm, dy, weights, wt, wo, send, keep, stats, wacc,
               prj, kr, vr, dat, att, gp, grads, scores, lows, done):
    project(nrm, dy, weights, wt, wo, prj, kr, vr, dat)
    attend(prj, kr, vr, dat, gp, att, scores, lows)
    patch = gp.shape[1]
    cols = pl.ds(pl.multiple_of(p * patch, patch), patch)
    grads[p] = mm(weights[0:D, :], gp[...]).astype(BF16)
    for copy in block_copies(core, p, send, keep, grads, done):
        copy.start()
    wacc[0:384] += mm(gp[...], nrm[...])
    wacc[384:512] += mm(att[...], dy[...])
    stats[0:1, cols] = jnp.sum(mm(weights[D:D + 16, :], gp[...]), axis=0, keepdims=True)
    stats[1:2, cols] = second_stat(gp, prj)


def second_stat(gp, prj):
    product = gp[...].astype(F32) * prj[...].astype(F32)
    queries = jnp.sum(product[0:128], axis=0, keepdims=True) * (1.0 / SCALE)
    return queries + jnp.sum(product[128:384], axis=0, keepdims=True)


def gather_rows(scal, order, points, cotangent, gain, own, slot, side, into_x, into_dy):
    patch = points.shape[1]
    half = patch // 2
    first = pl.multiple_of(scal[1] * 128, 128)
    chosen = one_hot_rows(order[pl.ds(slot, 1), half * side:half * side + half], patch)
    x = mm(chosen, points[slot]).astype(BF16)
    into_dy[...] = mm(chosen, cotangent[slot]).astype(BF16)
    own[...] = x
    normed, unit, inverse = norm_half(x, gain[...], own[:, pl.ds(first, 128)])
    into_x[...] = normed
    return unit, inverse


def local_kernel(scal, order, points, cotangent, gain, w3, wo,
                 send, keep, stats, unit_o, inv_o, wacc, weights, wt, nrm_o, dy_o,
                 nrm, dy, own, *work):
    half = points.shape[1] // 2
    for t in range(3):
        wt[128 * t:128 * t + 128, :] = w3[t].astype(F32).T.astype(BF16)
    wacc[...] = jnp.zeros_like(wacc)
    load_weights(w3, wt, gain, weights)

    whole = scal[2] > 1

    def step(p, carry):
        for side in range(2):
            rows = slice(half * side, half * side + half)

            @pl.when(jnp.logical_or(whole, p == side))
            def _():
                slot = jnp.where(whole, p + side, 0)
                unit, inverse = gather_rows(scal, order, points, cotangent, gain, own, slot,
                                            1 - side, nrm.at[rows], dy.at[rows])
                unit_o[p, :, rows] = unit
                inv_o[p, :, rows] = inverse

        @pl.when(whole)
        def _():
            patch_core(scal[0], p, nrm, dy, weights, wt, wo, send, keep, stats, wacc, *work)

        @pl.when(jnp.logical_not(whole))
        def _():
            here = pl.ds(pl.multiple_of(half * p, half), half)
            nrm_o[p] = nrm[here, :]
            dy_o[p] = dy[here, :]

        return carry

    lax.fori_loop(0, 2, step, 0)

    @pl.when(whole)
    def _():
        for p in range(2):
            for copy in block_copies(scal[0], p, send, keep, work[-4], work[-1]):
                copy.wait()


def cross_kernel(factor, scal, pull, pull_other, push, push_other, send_i, keep_i, wacc_i, nrm_i,
                 dy_i, stats_i, unit_i, inv_i, weights_i, wt_i, wo_i, gain,
                 send, keep, stats, unit_o, inv_o, pieces, gain_o, pushed,
                 flag, nrm_2, dy_2, own_2, weights, wt, wo, arrived, *work_wacc):
    wacc, work = work_wacc[-1], work_wacc[:-1]
    half = nrm_i.shape[1]
    part = half // 2
    first = pl.multiple_of(scal[1] * 128, 128)
    light = scal[2] == 1
    told = pltpu.make_async_copy(push.at[0, part:part + 16], flag, arrived.at[2, 0])
    told.start()
    copies = []
    common = ((stats_i, stats), (unit_i, unit_o), (inv_i, inv_o), (weights_i, weights), (wt_i, wt),
              (wo_i, wo))
    common = [pltpu.make_async_copy(source, into, arrived.at[2, k + 1])
              for k, (source, into) in enumerate(common)]
    for p, one, other in ((0, pull, pull_other), (1, push, push_other)):
        here, there = half * p, half * (1 - p)
        moves = [(nrm_i.at[p], nrm_2.at[p, here:here + half]),
                 (dy_i.at[p], dy_2.at[p, here:here + half])]
        for source, core in ((one, scal[0]), (other, 1 - scal[0])):
            at = pl.multiple_of(core * part, part)
            moves.append((source.at[0, 0:part], own_2.at[p, pl.ds(at, part)]))
            moves.append((source.at[1, 0:part],
                          dy_2.at[p, pl.ds(pl.multiple_of(there + at, part), part)]))
        copies.append([pltpu.make_async_copy(source, into, arrived.at[p, k])
                       for k, (source, into) in enumerate(moves)])
        for copy in copies[-1]:
            copy.start()
        if p == 0:
            for copy in common:
                copy.start()
    @pl.when(light)
    def _():
        wacc[...] = jnp.zeros_like(wacc)

    @pl.when(jnp.logical_not(light))
    def _():
        copy = pltpu.make_async_copy(wacc_i, wacc, arrived.at[3, 0])
        copy.start()
        copy.wait()

    told.wait()
    for copy in common:
        copy.wait()
    before = jnp.max(flag[...].astype(F32)).astype(jnp.int32)
    pushed[0] = before
    patches = jnp.where(light, jnp.where(before > 1, 2, 1), 0)

    def cross(p, carry):
        for q in range(2):
            @pl.when(p == q)
            def _():
                for copy in copies[q]:
                    copy.wait()

        @pl.when(p < patches)
        def _():
            there = pl.multiple_of(half * (1 - p), half)
            own = own_2.at[p]
            nrm = nrm_2.at[p]
            normed, unit, inverse = norm_half(own[...], gain[...], own[:, pl.ds(first, 128)])
            nrm[pl.ds(there, half), :] = normed
            unit_o[p, :, pl.ds(there, half)] = unit
            inv_o[p, :, pl.ds(there, half)] = inverse
            patch_core(scal[0], p, nrm, dy_2.at[p], weights, wt, wo, send, keep, stats, wacc,
                       *work)

        return carry

    lax.fori_loop(0, 2, cross, 0)
    total = wacc[0:384] * factor
    gain_o[...] = jnp.sum(total * wt[...].astype(F32), axis=0, keepdims=True) / gain[...]
    for r in range(16):
        for c in range(4):
            block = wacc[32 * r:32 * r + 32, 128 * c:128 * c + 128]
            pieces[4 * r + c] = (block * factor).astype(BF16)
    for p in range(2):
        @pl.when(p < patches)
        def _():
            for copy in block_copies(scal[0], p, send, keep, work[-4], work[-1]):
                copy.wait()


def pair_kernel(scal, keep, received, stats, stats_received, send, kept, stats_o):
    far = scal[3]
    send[...] = (keep[1 - far].astype(F32) + received[1 - far].astype(F32)).astype(BF16)
    kept[...] = (keep[far].astype(F32) + received[far].astype(F32)).astype(BF16)
    stats_o[...] = stats[...] + stats_received[...]


def branch_kernel(scal, kept, received, stats, stats_received, unit, stat, gain,
                  branch, back, ahead):
    half = branch.shape[2] // 2
    own_gain = gain[:, pl.ds(pl.multiple_of(scal[1] * 128, 128), 128)]
    own_gain = jnp.broadcast_to(own_gain, (128, 128)).T[:, 0:1]
    scaled = (kept[...].astype(F32) + received[...].astype(F32)) * own_gain
    mean = (stats[0:1, :] + stats_received[0:1, :]) * (1.0 / D)
    slope = (stats[1:2, :] + stats_received[1:2, :]) * (1.0 / D)
    rows = (stat[0, 0:1, :] * (scaled - mean - unit[0].astype(F32) * slope)).astype(BF16)
    branch[0] = rows

    @pl.when(pl.program_id(0) == 0)
    def _():
        ahead[...] = rows[:, half:]

    @pl.when(pl.program_id(0) == 1)
    def _():
        back[...] = rows[:, :half]


def total_kernel(scal, received, gain, gain_received, out):
    def add(i, total):
        return total + received[i].astype(F32)

    total = lax.fori_loop(0, received.shape[0], add, jnp.zeros(received.shape[1:], F32), unroll=8)
    low = total.astype(BF16)
    at = pl.ds(pl.multiple_of(scal[1] * 128, 128), 128)
    own_gain = jnp.broadcast_to(gain[:, at] + gain_received[:, at], (8, 128)).astype(BF16)

    def put(i, carry):
        out[i, 0:32, :] = low
        out[i, 32:40, :] = own_gain
        return carry

    lax.fori_loop(0, received.shape[0], put, 0, unroll=8)


def place_kernel(scal, order, before, cotangent, branch, from_before, from_after, out, placed):
    slot = pl.program_id(0)
    count = scal[2]
    patch = out.shape[1]
    half = patch // 2

    @pl.when(slot >= count)
    def _():
        out[...] = cotangent[...]

    @pl.when(slot < count)
    def _():
        local = before[0] > 1

        @pl.when(jnp.logical_and(slot == 0, jnp.logical_not(local)))
        def _():
            placed[:, 0:half] = from_before[...]

        @pl.when(jnp.logical_and(slot == 0, local))
        def _():
            placed[:, 0:half] = branch[1, :, half:]

        @pl.when(slot > 0)
        def _():
            placed[:, 0:half] = branch[jnp.maximum(slot - 1, 0), :, half:]

        @pl.when(slot < 2)
        def _():
            placed[:, half:] = branch[jnp.minimum(slot, 1), :, 0:half]

        @pl.when(slot == 2)
        def _():
            placed[:, half:] = from_after[...]

        places = order[pl.ds(slot, 1), :]
        rows = 256
        for r in range(patch // rows):
            index = lax.broadcasted_iota(jnp.int32, (rows, patch), 0) + rows * r
            chosen = (index == places).astype(BF16)
            moved = mm_nt(chosen, placed[...])
            own = cotangent[0, rows * r:rows * r + rows, :].astype(F32)
            out[0, rows * r:rows * r + rows, :] = (own + moved).astype(BF16)


def finish_kernel(received, qkv, out, gain):
    gain[...] = jnp.sum(received[:, 32:40, :].astype(F32), axis=0)[0:1]
    for t in range(3):
        for c in range(4):
            block = jnp.concatenate(
                [received[4 * (4 * t + r) + c, 0:32, :].astype(F32) for r in range(4)], axis=0
            )
            qkv[t, 128 * c:128 * c + 128, :] = block.T
    for r in range(4):
        for c in range(4):
            out[32 * r:32 * r + 32, 128 * c:128 * c + 128] = received[
                4 * (12 + r) + c, 0:32, :
            ].astype(F32)


def shards(points, order, counts, cotangent, norm_gain, w_qkv, w_out):
    slots, patch, width = points.shape
    half = patch // 2
    curve = lax.axis_size("curve")
    model_part = lax.axis_index("mp")
    core = model_part % 2
    far = model_part // 2
    scal = jnp.stack([core, model_part, counts[0], far]).astype(jnp.int32)
    gain_row = norm_gain.reshape(1, width)
    w3 = jnp.transpose(w_qkv, (1, 0, 2))
    sds = jax.ShapeDtypeStruct

    def passed(x, by):
        return lax.ppermute(x, "curve", [(i, (i + by) % curve) for i in range(curve)])

    def swapped(x, bit):
        return lax.ppermute(x, "mp", [(i, i ^ bit) for i in range(4)])

    pull, push = pl.pallas_call(
        halo_kernel,
        in_specs=[SMEM, ANY, ANY, ANY],
        out_specs=[VMEM] * 2,
        out_shape=[sds((2, half // 2, width), BF16), sds((2, half // 2 + 16, width), BF16)],
        scratch_shapes=[
            pltpu.VMEM((slots, patch), jnp.int32),
            pltpu.VMEM((4, patch, width), BF16),
            pltpu.SemaphoreType.DMA((5,)),
        ],
        compiler_params=params(60),
        name="halo",
    )(counts, order, points, cotangent)
    pull, push = passed(pull, -1), passed(push, 1)

    rows = [
        pltpu.VMEM((patch, width), BF16),
        pltpu.VMEM((patch, width), BF16),
        pltpu.VMEM((half, width), BF16),
    ]
    rows_2 = [
        pltpu.VMEM((16, width), BF16),
        pltpu.VMEM((2, patch, width), BF16),
        pltpu.VMEM((2, patch, width), BF16),
        pltpu.VMEM((2, half, width), BF16),
        pltpu.VMEM((width + 16, 384), BF16),
        pltpu.VMEM((384, width), BF16),
        pltpu.VMEM((128, width), BF16),
        pltpu.SemaphoreType.DMA((4, 7)),
    ]
    work = [
        pltpu.VMEM((384, patch), BF16),
        pltpu.VMEM((patch, 128), BF16),
        pltpu.VMEM((patch, 128), BF16),
        pltpu.VMEM((128, patch), BF16),
        pltpu.VMEM((128, patch), BF16),
        pltpu.VMEM((384, patch), BF16),
        pltpu.VMEM((2, width, patch), BF16),
        pltpu.VMEM((2, patch, patch), F32),
        pltpu.VMEM((2, patch, patch), BF16),
        pltpu.SemaphoreType.DMA((2, 4)),
    ]
    lanes = 2 * patch
    shared = [
        sds((2, 128, lanes), BF16),
        sds((2, 128, lanes), BF16),
        sds((2, lanes), F32),
        sds((2, 128, patch), BF16),
        sds((2, 8, patch), F32),
    ]
    send, keep, stats, unit, inverse, wacc, weights, wt, nrm, dy = pl.pallas_call(
        local_kernel,
        in_specs=[SMEM] + [VMEM] * 6,
        out_specs=[ANY] * 2 + [VMEM] * 8,
        out_shape=shared + [
            sds((512, width), F32),
            sds((width + 16, 384), BF16),
            sds((384, width), BF16),
            sds((2, half, width), BF16),
            sds((2, half, width), BF16),
        ],
        scratch_shapes=rows + work,
        compiler_params=params(60),
        cost_estimate=cost(16 * 10**9, 16 * 10**6),
        name="local",
    )(scal, order, points, cotangent, gain_row, w3, w_out)
    pull, wacc = lax.optimization_barrier((pull, wacc))
    pull_other = swapped(pull, 1)
    push, pull_other = lax.optimization_barrier((push, pull_other))
    push_other = swapped(push, 1)

    factor = 1.0 / math.sqrt(curve * slots * patch)
    send, keep, stats, unit, inverse, pieces, gain_part, before = pl.pallas_call(
        functools.partial(cross_kernel, factor),
        in_specs=[SMEM] + [HBM] * 15 + [VMEM],
        out_specs=[ANY] * 2 + [VMEM] * 5 + [SMEM],
        out_shape=shared + [
            sds((64, 32, 128), BF16), sds((1, width), F32), sds((1,), jnp.int32)
        ],
        scratch_shapes=rows_2 + work + [pltpu.VMEM((512, width), F32)],
        input_output_aliases={5: 0, 6: 1},
        compiler_params=params(60),
        cost_estimate=cost(4 * 10**9, 8 * 10**6),
        name="cross",
    )(scal, pull, pull_other, push, push_other, send, keep, wacc, nrm, dy, stats, unit,
      inverse, weights, wt, w_out, gain_row)

    received = lax.all_to_all(pieces, "curve", 0, 0)
    gain_part = gain_part + swapped(gain_part, 1)
    gain_far = swapped(gain_part, 2)

    def whole(*shape):
        return pl.BlockSpec(shape, lambda i: (0,) * len(shape))

    def by_patch(*shape):
        return pl.BlockSpec((1,) + shape, lambda i: (i,) + (0,) * len(shape))

    def by_lanes(*shape):
        return pl.BlockSpec(shape + (patch,), lambda i: (0,) * len(shape) + (i,))

    near, near_stats = swapped(send, 1), swapped(stats, 1)
    send, kept, stats = pl.pallas_call(
        pair_kernel,
        grid=(2,),
        in_specs=[SMEM, by_lanes(2, 128), by_lanes(2, 128), by_lanes(2), by_lanes(2)],
        out_specs=[by_lanes(128), by_lanes(128), by_lanes(2)],
        out_shape=[sds((128, lanes), BF16), sds((128, lanes), BF16), sds((2, lanes), F32)],
        compiler_params=params(16),
        cost_estimate=cost(1000, 1000),
        name="pair",
    )(scal, keep, near, stats, near_stats)
    send, gain_far = lax.optimization_barrier((send, gain_far))
    away, away_stats = swapped(send, 2), swapped(stats, 2)
    branch, back, ahead = pl.pallas_call(
        branch_kernel,
        grid=(2,),
        in_specs=[SMEM, by_lanes(128), by_lanes(128), by_lanes(2), by_lanes(2),
                  by_patch(128, patch), by_patch(8, patch), whole(1, width)],
        out_specs=[by_patch(128, patch), whole(128, half), whole(128, half)],
        out_shape=[sds((2, 128, patch), BF16), sds((128, half), BF16), sds((128, half), BF16)],
        compiler_params=params(16),
        cost_estimate=cost(10**10, 1000),
        name="branch",
    )(scal, kept, away, stats, away_stats, unit, inverse, gain_row)
    from_before, from_after = passed(ahead, 1), passed(back, -1)

    totals = pl.pallas_call(
        total_kernel,
        in_specs=[SMEM] + [VMEM] * 3,
        out_specs=VMEM,
        out_shape=sds((64, 40, 128), BF16),
        compiler_params=params(16),
        name="total",
    )(scal, received, gain_part, gain_far)
    gathered = lax.all_to_all(totals, "curve", 0, 0)

    grad_points = pl.pallas_call(
        place_kernel,
        grid_spec=pltpu.PrefetchScalarGridSpec(
            num_scalar_prefetch=1,
            grid=(slots,),
            in_specs=[
                pl.BlockSpec((slots, patch), lambda i, s: (0, 0)),
                SMEM,
                pl.BlockSpec((1, patch, 128), lambda i, s: (i, 0, s[1])),
                pl.BlockSpec((2, 128, patch), lambda i, s: (0, 0, 0)),
                pl.BlockSpec((128, half), lambda i, s: (0, 0)),
                pl.BlockSpec((128, half), lambda i, s: (0, 0)),
            ],
            out_specs=pl.BlockSpec((1, patch, 128), lambda i, s: (i, 0, 0)),
            scratch_shapes=[pltpu.VMEM((128, patch), BF16)],
        ),
        out_shape=sds((slots, patch, 128), BF16),
        compiler_params=params(16),
        cost_estimate=cost(10**10, 1000),
        name="place",
    )(scal, order, before, cotangent, branch, from_before, from_after)

    grad_qkv, grad_out, grad_gain = pl.pallas_call(
        finish_kernel,
        in_specs=[VMEM],
        out_specs=[VMEM] * 3,
        out_shape=[sds((3, width, 128), F32), sds((128, width), F32), sds((1, 128), F32)],
        compiler_params=params(16),
        name="finish",
    )(gathered)
    return grad_points, grad_gain.reshape(128), jnp.transpose(grad_qkv, (1, 0, 2)), grad_out


def solution(mesh):
    in_specs = (
        P("curve", None, None),
        P("curve", None),
        P("curve"),
        P("curve", None, None),
        P(),
        P(None, None, "mp"),
        P("mp", None),
    )
    out_specs = (P("curve", None, "mp"), P("mp"), P(None, None, "mp"), P("mp", None))
    return jax.shard_map(shards, mesh=mesh, in_specs=in_specs, out_specs=out_specs, check_vma=False)
```

```python
import functools
import math

import jax
import jax.numpy as jnp
from jax import lax
from jax.experimental import pallas as pl
from jax.experimental.pallas import tpu as pltpu
from jax.sharding import PartitionSpec as P

D = 512
HEADS = 8
HEAD = D // HEADS
EPSILON = 1e-05
SCALE = HEAD ** (-0.5) * math.log2(math.e)

F32 = jnp.float32
BF16 = jnp.bfloat16
NT = (((1,), (1,)), ((), ()))
VMEM = pl.BlockSpec(memory_space=pltpu.VMEM)
SMEM = pl.BlockSpec(memory_space=pltpu.SMEM)
ANY = pl.BlockSpec(memory_space=pl.ANY)
HBM = pl.BlockSpec(memory_space=pltpu.HBM)


def mm(a, b):
    return jnp.dot(a, b, preferred_element_type=F32)


def mm_nt(a, b):
    return lax.dot_general(a, b, NT, preferred_element_type=F32)


def params(mib):
    return pltpu.CompilerParams(vmem_limit_bytes=mib * 1024 * 1024)


def cost(flops, bytes_accessed):
    return pl.CostEstimate(flops=flops, bytes_accessed=bytes_accessed, transcendentals=0)


def one_hot_rows(places, patch):
    count = places.shape[1]
    column = jnp.broadcast_to(places, (128, count)).T
    lanes = lax.broadcasted_iota(jnp.int32, (count, 128), 1)
    return jnp.concatenate(
        [(column == lanes + 128 * b).astype(BF16) for b in range(patch // 128)], axis=1
    )


def halo_kernel(counts, order_i, points, cotangent, pull, push, order, held, done):
    rows = pull.shape[1]
    patch = points.shape[1]
    last = points.shape[0] - 1
    core = lax.axis_index("mp") % 2
    places = pltpu.make_async_copy(order_i, order, done.at[4])
    places.start()
    copies = []
    for slot in (last, 0):
        for source in (points, cotangent):
            k = len(copies)
            copies.append(pltpu.make_async_copy(source.at[slot], held.at[k], done.at[k]))
            copies[-1].start()
    count = jnp.zeros((16, push.shape[2]), F32) + counts[0].astype(F32)
    push[0, rows:, :] = count.astype(BF16)
    push[1, rows:, :] = count.astype(BF16)
    places.wait()
    for k, (slot, base, out) in enumerate(((last, patch // 2, push), (0, 0, pull))):
        at = pl.ds(pl.multiple_of(base + core * rows, rows), rows)
        chosen = one_hot_rows(order[slot:slot + 1, at], patch)
        for j in range(2):
            copies[2 * k + j].wait()
            out[j, 0:rows, :] = mm(chosen, held[2 * k + j]).astype(BF16)


def norm_half(x, gain, own):
    values = x.astype(F32)
    mean = jnp.mean(values, axis=1, keepdims=True)
    centre = values - mean
    inverse = lax.rsqrt(jnp.mean(centre * centre, axis=1, keepdims=True) + EPSILON)
    normed = (centre * inverse * gain).astype(BF16)
    unit = ((own.astype(F32) - mean) * inverse).T.astype(BF16)
    inverse_row = jnp.broadcast_to(inverse, (x.shape[0], 128)).T[0:8]
    return normed, unit, inverse_row


def project(nrm, dy, weights, wt, wo, prj, kr, vr, dat):
    prj[0:128, :] = (mm_nt(wt[0:128, :], nrm[...]) * SCALE).astype(BF16)
    prj[128:384, :] = mm_nt(wt[128:384, :], nrm[...]).astype(BF16)
    both = mm(nrm[...], weights[0:D, 128:384]).astype(BF16)
    kr[...] = both[:, 0:128]
    vr[...] = both[:, 128:256]
    dat[...] = mm_nt(wo[...], dy[...]).astype(BF16)


def attend(prj, kr, vr, dat, gp, att, scores, lows):
    patch = prj.shape[1]
    chunk = 256
    blocks = [slice(c, c + chunk) for c in range(0, patch, chunk)]
    zeros = jnp.zeros((HEAD, patch), BF16)
    state = [{}, {}]

    def pad(x, h):
        return jnp.concatenate([x, zeros] if h == 0 else [zeros, x], axis=0)

    def fold(x, op):
        return op(x.reshape(chunk // 8, 8, patch), axis=0)

    def score(h, keys):
        here, lo = state[h], h * HEAD
        block = mm(kr[keys, :], pad(prj[lo:lo + HEAD, :], h))
        scores[h, keys, :] = block
        high = fold(block, jnp.max)
        here["high"] = jnp.maximum(here["high"], high) if "high" in here else high
        if keys.stop == patch:
            here["high"] = jnp.max(here["high"], axis=0, keepdims=True)

    def soften(h, keys):
        here, lo = state[h], h * HEAD
        expos = jnp.exp2(scores[h, keys, :] - here["high"])
        scores[h, keys, :] = expos
        lows[h, keys, :] = expos.astype(BF16)
        total = fold(expos, jnp.sum)
        here["total"] = here["total"] + total if "total" in here else total
        if keys.stop == patch:
            recip = 1.0 / jnp.sum(here["total"], axis=0, keepdims=True)
            attended = mm(prj[256 + lo:256 + lo + HEAD, :], lows[h]) * recip
            att[lo:lo + HEAD, :] = attended.astype(BF16)
            grad = dat[lo:lo + HEAD, :].astype(F32) * recip
            here["inner"] = jnp.sum(grad * attended, axis=0, keepdims=True)
            here["grad"] = grad.astype(BF16)

    def back(h, keys):
        here, lo = state[h], h * HEAD
        grad_probs = mm(vr[keys, :], pad(here["grad"], h))
        grad_scores = (scores[h, keys, :] * (grad_probs - here["inner"])).astype(BF16)
        dk = mm_nt(prj[lo:lo + HEAD, :], grad_scores) * (HEAD ** (-0.5) / SCALE)
        gp[128 + lo:128 + lo + HEAD, keys] = dk.astype(BF16)
        gp[256 + lo:256 + lo + HEAD, keys] = mm_nt(here["grad"], lows[h, keys, :]).astype(BF16)
        lows[h, keys, :] = grad_scores
        if keys.stop == patch:
            dq = mm(prj[128 + lo:128 + lo + HEAD, :], lows[h]) * (HEAD ** (-0.5))
            gp[lo:lo + HEAD, :] = dq.astype(BF16)

    for keys in blocks:
        score(0, keys)
    for keys in blocks:
        score(1, keys)
        soften(0, keys)
    for keys in blocks:
        back(0, keys)
        soften(1, keys)
    for keys in blocks:
        back(1, keys)


def split3(x):
    first = x.astype(BF16)
    rest = x - first.astype(F32)
    second = rest.astype(BF16)
    third = (rest - second.astype(F32)).astype(BF16)
    none = jnp.zeros((13, x.shape[1]), BF16)
    return jnp.concatenate([first, second, third, none], axis=0)


def load_weights(w3, wt, gain, weights):
    for t in range(3):
        weights[0:D, 128 * t:128 * t + 128] = w3[t]
    sums = jnp.sum(mm_nt(split3(gain[...]), wt[...]), axis=0, keepdims=True)
    weights[D:D + 16, :] = split3(sums)


def block_copies(core, p, send, keep, grads, done):
    patch = grads.shape[2]
    cols = pl.ds(pl.multiple_of(p * patch, patch), patch)
    copies = []
    for j in range(2):
        for k, (block, into) in enumerate(((2 * j + 1 - core, send), (2 * j + core, keep))):
            rows = pl.ds(pl.multiple_of(block * 128, 128), 128)
            copies.append(pltpu.make_async_copy(
                grads.at[p, rows], into.at[j, :, cols], done.at[p, 2 * j + k]
            ))
    return copies


def patch_core(core, p, nrm, dy, weights, wt, wo, send, keep, stats, wacc,
               prj, kr, vr, dat, att, gp, grads, scores, lows, done):
    project(nrm, dy, weights, wt, wo, prj, kr, vr, dat)
    attend(prj, kr, vr, dat, gp, att, scores, lows)
    patch = gp.shape[1]
    cols = pl.ds(pl.multiple_of(p * patch, patch), patch)
    grads[p] = mm(weights[0:D, :], gp[...]).astype(BF16)
    for copy in block_copies(core, p, send, keep, grads, done):
        copy.start()
    wacc[0:384] += mm(gp[...], nrm[...])
    wacc[384:512] += mm(att[...], dy[...])
    stats[0:1, cols] = jnp.sum(mm(weights[D:D + 16, :], gp[...]), axis=0, keepdims=True)
    stats[1:2, cols] = second_stat(gp, prj)


def second_stat(gp, prj):
    product = gp[...].astype(F32) * prj[...].astype(F32)
    queries = jnp.sum(product[0:128], axis=0, keepdims=True) * (1.0 / SCALE)
    return queries + jnp.sum(product[128:384], axis=0, keepdims=True)


def gather_rows(scal, order, points, cotangent, gain, own, slot, side, into_x, into_dy):
    patch = points.shape[1]
    half = patch // 2
    first = pl.multiple_of(scal[1] * 128, 128)
    chosen = one_hot_rows(order[pl.ds(slot, 1), half * side:half * side + half], patch)
    x = mm(chosen, points[slot]).astype(BF16)
    into_dy[...] = mm(chosen, cotangent[slot]).astype(BF16)
    own[...] = x
    normed, unit, inverse = norm_half(x, gain[...], own[:, pl.ds(first, 128)])
    into_x[...] = normed
    return unit, inverse


def local_kernel(scal, order, points, cotangent, gain, w3, wo,
                 send, keep, stats, unit_o, inv_o, wacc, weights, wt, nrm_o, dy_o,
                 nrm, dy, own, *work):
    half = points.shape[1] // 2
    for t in range(3):
        wt[128 * t:128 * t + 128, :] = w3[t].astype(F32).T.astype(BF16)
    wacc[...] = jnp.zeros_like(wacc)
    load_weights(w3, wt, gain, weights)

    whole = scal[2] > 1

    def step(p, carry):
        for side in range(2):
            rows = slice(half * side, half * side + half)

            @pl.when(jnp.logical_or(whole, p == side))
            def _():
                slot = jnp.where(whole, p + side, 0)
                unit, inverse = gather_rows(scal, order, points, cotangent, gain, own, slot,
                                            1 - side, nrm.at[rows], dy.at[rows])
                unit_o[p, :, rows] = unit
                inv_o[p, :, rows] = inverse

        @pl.when(whole)
        def _():
            patch_core(scal[0], p, nrm, dy, weights, wt, wo, send, keep, stats, wacc, *work)

        @pl.when(jnp.logical_not(whole))
        def _():
            here = pl.ds(pl.multiple_of(half * p, half), half)
            copies = [pltpu.make_async_copy(nrm.at[here], nrm_o.at[p], work[-1].at[p, 0]),
                      pltpu.make_async_copy(dy.at[here], dy_o.at[p], work[-1].at[p, 1])]
            for copy in copies:
                copy.start()
            for copy in copies:
                copy.wait()

        return carry

    lax.fori_loop(0, 2, step, 0)

    @pl.when(whole)
    def _():
        for p in range(2):
            for copy in block_copies(scal[0], p, send, keep, work[-4], work[-1]):
                copy.wait()


def cross_kernel(factor, scal, pull, pull_other, push, push_other, send_i, keep_i, wacc_i, nrm_i,
                 dy_i, stats_i, unit_i, inv_i, weights_i, wt_i, wo_i, gain,
                 send, keep, stats, unit_o, inv_o, pieces, gain_o, pushed,
                 flag, nrm_2, dy_2, own_2, weights, wt, wo, arrived, *work_wacc):
    wacc, work = work_wacc[-1], work_wacc[:-1]
    half = nrm_i.shape[1]
    part = half // 2
    first = pl.multiple_of(scal[1] * 128, 128)
    light = scal[2] == 1
    told = pltpu.make_async_copy(push.at[0, part:part + 16], flag, arrived.at[2, 0])
    told.start()
    copies = []
    common = ((stats_i, stats), (unit_i, unit_o), (inv_i, inv_o), (weights_i, weights), (wt_i, wt),
              (wo_i, wo))
    common = [pltpu.make_async_copy(source, into, arrived.at[2, k + 1])
              for k, (source, into) in enumerate(common)]
    for p, one, other in ((0, pull, pull_other), (1, push, push_other)):
        here, there = half * p, half * (1 - p)
        moves = [(nrm_i.at[p], nrm_2.at[p, here:here + half]),
                 (dy_i.at[p], dy_2.at[p, here:here + half])]
        for source, core in ((one, scal[0]), (other, 1 - scal[0])):
            at = pl.multiple_of(core * part, part)
            moves.append((source.at[0, 0:part], own_2.at[p, pl.ds(at, part)]))
            moves.append((source.at[1, 0:part],
                          dy_2.at[p, pl.ds(pl.multiple_of(there + at, part), part)]))
        copies.append([pltpu.make_async_copy(source, into, arrived.at[p, k])
                       for k, (source, into) in enumerate(moves)])
        for copy in copies[-1]:
            copy.start()
        if p == 0:
            for copy in common:
                copy.start()
    @pl.when(light)
    def _():
        wacc[...] = jnp.zeros_like(wacc)

    @pl.when(jnp.logical_not(light))
    def _():
        copy = pltpu.make_async_copy(wacc_i, wacc, arrived.at[3, 0])
        copy.start()
        copy.wait()

    told.wait()
    for copy in common:
        copy.wait()
    before = jnp.max(flag[...].astype(F32)).astype(jnp.int32)
    pushed[0] = before
    patches = jnp.where(light, jnp.where(before > 1, 2, 1), 0)

    def cross(p, carry):
        for q in range(2):
            @pl.when(p == q)
            def _():
                for copy in copies[q]:
                    copy.wait()

        @pl.when(p < patches)
        def _():
            there = pl.multiple_of(half * (1 - p), half)
            own = own_2.at[p]
            nrm = nrm_2.at[p]
            normed, unit, inverse = norm_half(own[...], gain[...], own[:, pl.ds(first, 128)])
            nrm[pl.ds(there, half), :] = normed
            unit_o[p, :, pl.ds(there, half)] = unit
            inv_o[p, :, pl.ds(there, half)] = inverse
            patch_core(scal[0], p, nrm, dy_2.at[p], weights, wt, wo, send, keep, stats, wacc,
                       *work)

        return carry

    lax.fori_loop(0, 2, cross, 0)
    total = wacc[0:384] * factor
    gain_o[...] = jnp.sum(total * wt[...].astype(F32), axis=0, keepdims=True) / gain[...]
    for r in range(16):
        for c in range(4):
            block = wacc[32 * r:32 * r + 32, 128 * c:128 * c + 128]
            pieces[4 * r + c] = (block * factor).astype(BF16)
    for p in range(2):
        @pl.when(p < patches)
        def _():
            for copy in block_copies(scal[0], p, send, keep, work[-4], work[-1]):
                copy.wait()


def pair_kernel(scal, keep, received, stats, stats_received, send, kept, stats_o):
    far = scal[3]
    send[...] = (keep[1 - far].astype(F32) + received[1 - far].astype(F32)).astype(BF16)
    kept[...] = (keep[far].astype(F32) + received[far].astype(F32)).astype(BF16)
    stats_o[...] = stats[...] + stats_received[...]


def branch_kernel(scal, kept, received, stats, stats_received, unit, stat, gain,
                  branch, back, ahead):
    half = branch.shape[2] // 2
    own_gain = gain[:, pl.ds(pl.multiple_of(scal[1] * 128, 128), 128)]
    own_gain = jnp.broadcast_to(own_gain, (128, 128)).T[:, 0:1]
    scaled = (kept[...].astype(F32) + received[...].astype(F32)) * own_gain
    mean = (stats[0:1, :] + stats_received[0:1, :]) * (1.0 / D)
    slope = (stats[1:2, :] + stats_received[1:2, :]) * (1.0 / D)
    rows = (stat[0, 0:1, :] * (scaled - mean - unit[0].astype(F32) * slope)).astype(BF16)
    branch[0] = rows

    @pl.when(pl.program_id(0) == 0)
    def _():
        ahead[...] = rows[:, half:]

    @pl.when(pl.program_id(0) == 1)
    def _():
        back[...] = rows[:, :half]


def total_kernel(scal, received, gain, gain_received, out):
    def add(i, total):
        return total + received[i].astype(F32)

    total = lax.fori_loop(0, received.shape[0], add, jnp.zeros(received.shape[1:], F32), unroll=8)
    low = total.astype(BF16)
    at = pl.ds(pl.multiple_of(scal[1] * 128, 128), 128)
    own_gain = jnp.broadcast_to(gain[:, at] + gain_received[:, at], (8, 128)).astype(BF16)

    def put(i, carry):
        out[i, 0:32, :] = low
        out[i, 32:40, :] = own_gain
        return carry

    lax.fori_loop(0, received.shape[0], put, 0, unroll=8)


def place_kernel(scal, order, before, cotangent, branch, from_before, from_after, out, placed):
    slot = pl.program_id(0)
    count = scal[2]
    patch = out.shape[1]
    half = patch // 2

    @pl.when(slot >= count)
    def _():
        out[...] = cotangent[...]

    @pl.when(slot < count)
    def _():
        local = before[0] > 1

        @pl.when(jnp.logical_and(slot == 0, jnp.logical_not(local)))
        def _():
            placed[:, 0:half] = from_before[...]

        @pl.when(jnp.logical_and(slot == 0, local))
        def _():
            placed[:, 0:half] = branch[1, :, half:]

        @pl.when(slot > 0)
        def _():
            placed[:, 0:half] = branch[jnp.maximum(slot - 1, 0), :, half:]

        @pl.when(slot < 2)
        def _():
            placed[:, half:] = branch[jnp.minimum(slot, 1), :, 0:half]

        @pl.when(slot == 2)
        def _():
            placed[:, half:] = from_after[...]

        places = order[pl.ds(slot, 1), :]
        rows = 256
        for r in range(patch // rows):
            index = lax.broadcasted_iota(jnp.int32, (rows, patch), 0) + rows * r
            chosen = (index == places).astype(BF16)
            moved = mm_nt(chosen, placed[...])
            own = cotangent[0, rows * r:rows * r + rows, :].astype(F32)
            out[0, rows * r:rows * r + rows, :] = (own + moved).astype(BF16)


def finish_kernel(received, qkv, out, gain):
    gain[...] = jnp.sum(received[:, 32:40, :].astype(F32), axis=0)[0:1]
    for t in range(3):
        for c in range(4):
            block = jnp.concatenate(
                [received[4 * (4 * t + r) + c, 0:32, :].astype(F32) for r in range(4)], axis=0
            )
            qkv[t, 128 * c:128 * c + 128, :] = block.T
    for r in range(4):
        for c in range(4):
            out[32 * r:32 * r + 32, 128 * c:128 * c + 128] = received[
                4 * (12 + r) + c, 0:32, :
            ].astype(F32)


def shards(points, order, counts, cotangent, norm_gain, w_qkv, w_out):
    slots, patch, width = points.shape
    half = patch // 2
    curve = lax.axis_size("curve")
    model_part = lax.axis_index("mp")
    core = model_part % 2
    far = model_part // 2
    scal = jnp.stack([core, model_part, counts[0], far]).astype(jnp.int32)
    gain_row = norm_gain.reshape(1, width)
    w3 = jnp.transpose(w_qkv, (1, 0, 2))
    sds = jax.ShapeDtypeStruct

    def passed(x, by):
        return lax.ppermute(x, "curve", [(i, (i + by) % curve) for i in range(curve)])

    def swapped(x, bit):
        return lax.ppermute(x, "mp", [(i, i ^ bit) for i in range(4)])

    pull, push = pl.pallas_call(
        halo_kernel,
        in_specs=[SMEM, ANY, ANY, ANY],
        out_specs=[VMEM] * 2,
        out_shape=[sds((2, half // 2, width), BF16), sds((2, half // 2 + 16, width), BF16)],
        scratch_shapes=[
            pltpu.VMEM((slots, patch), jnp.int32),
            pltpu.VMEM((4, patch, width), BF16),
            pltpu.SemaphoreType.DMA((5,)),
        ],
        compiler_params=params(60),
        name="halo",
    )(counts, order, points, cotangent)
    pull, push = passed(pull, -1), passed(push, 1)

    rows = [
        pltpu.VMEM((patch, width), BF16),
        pltpu.VMEM((patch, width), BF16),
        pltpu.VMEM((half, width), BF16),
    ]
    rows_2 = [
        pltpu.VMEM((16, width), BF16),
        pltpu.VMEM((2, patch, width), BF16),
        pltpu.VMEM((2, patch, width), BF16),
        pltpu.VMEM((2, half, width), BF16),
        pltpu.VMEM((width + 16, 384), BF16),
        pltpu.VMEM((384, width), BF16),
        pltpu.VMEM((128, width), BF16),
        pltpu.SemaphoreType.DMA((4, 7)),
    ]
    work = [
        pltpu.VMEM((384, patch), BF16),
        pltpu.VMEM((patch, 128), BF16),
        pltpu.VMEM((patch, 128), BF16),
        pltpu.VMEM((128, patch), BF16),
        pltpu.VMEM((128, patch), BF16),
        pltpu.VMEM((384, patch), BF16),
        pltpu.VMEM((2, width, patch), BF16),
        pltpu.VMEM((2, patch, patch), F32),
        pltpu.VMEM((2, patch, patch), BF16),
        pltpu.SemaphoreType.DMA((2, 4)),
    ]
    lanes = 2 * patch
    shared = [
        sds((2, 128, lanes), BF16),
        sds((2, 128, lanes), BF16),
        sds((2, lanes), F32),
        sds((2, 128, patch), BF16),
        sds((2, 8, patch), F32),
    ]
    send, keep, stats, unit, inverse, wacc, weights, wt, nrm, dy = pl.pallas_call(
        local_kernel,
        in_specs=[SMEM] + [VMEM] * 6,
        out_specs=[ANY] * 2 + [VMEM] * 6 + [ANY] * 2,
        out_shape=shared + [
            sds((512, width), F32),
            sds((width + 16, 384), BF16),
            sds((384, width), BF16),
            sds((2, half, width), BF16),
            sds((2, half, width), BF16),
        ],
        scratch_shapes=rows + work,
        compiler_params=params(60),
        cost_estimate=cost(16 * 10**9, 16 * 10**6),
        name="local",
    )(scal, order, points, cotangent, gain_row, w3, w_out)
    pull, push, wacc = lax.optimization_barrier((pull, push, wacc))

    factor = 1.0 / math.sqrt(curve * slots * patch)
    send, keep, stats, unit, inverse, pieces, gain_part, before = pl.pallas_call(
        functools.partial(cross_kernel, factor),
        in_specs=[SMEM] + [HBM] * 15 + [VMEM],
        out_specs=[ANY] * 2 + [VMEM] * 5 + [SMEM],
        out_shape=shared + [
            sds((64, 32, 128), BF16), sds((1, width), F32), sds((1,), jnp.int32)
        ],
        scratch_shapes=rows_2 + work + [pltpu.VMEM((512, width), F32)],
        input_output_aliases={5: 0, 6: 1},
        compiler_params=params(60),
        cost_estimate=cost(4 * 10**9, 8 * 10**6),
        name="cross",
    )(scal, pull, swapped(pull, 1), push, swapped(push, 1), send, keep, wacc, nrm, dy, stats, unit,
      inverse, weights, wt, w_out, gain_row)

    received = lax.all_to_all(pieces, "curve", 0, 0)
    gain_part = gain_part + swapped(gain_part, 1)
    gain_far = swapped(gain_part, 2)

    def whole(*shape):
        return pl.BlockSpec(shape, lambda i: (0,) * len(shape))

    def by_patch(*shape):
        return pl.BlockSpec((1,) + shape, lambda i: (i,) + (0,) * len(shape))

    def by_lanes(*shape):
        return pl.BlockSpec(shape + (patch,), lambda i: (0,) * len(shape) + (i,))

    near, near_stats = swapped(send, 1), swapped(stats, 1)
    send, kept, stats = pl.pallas_call(
        pair_kernel,
        grid=(2,),
        in_specs=[SMEM, by_lanes(2, 128), by_lanes(2, 128), by_lanes(2), by_lanes(2)],
        out_specs=[by_lanes(128), by_lanes(128), by_lanes(2)],
        out_shape=[sds((128, lanes), BF16), sds((128, lanes), BF16), sds((2, lanes), F32)],
        compiler_params=params(16),
        cost_estimate=cost(1000, 1000),
        name="pair",
    )(scal, keep, near, stats, near_stats)
    send, gain_far = lax.optimization_barrier((send, gain_far))
    away, away_stats = swapped(send, 2), swapped(stats, 2)
    branch, back, ahead = pl.pallas_call(
        branch_kernel,
        grid=(2,),
        in_specs=[SMEM, by_lanes(128), by_lanes(128), by_lanes(2), by_lanes(2),
                  by_patch(128, patch), by_patch(8, patch), whole(1, width)],
        out_specs=[by_patch(128, patch), whole(128, half), whole(128, half)],
        out_shape=[sds((2, 128, patch), BF16), sds((128, half), BF16), sds((128, half), BF16)],
        compiler_params=params(16),
        cost_estimate=cost(10**10, 1000),
        name="branch",
    )(scal, kept, away, stats, away_stats, unit, inverse, gain_row)
    from_before, from_after = passed(ahead, 1), passed(back, -1)

    totals = pl.pallas_call(
        total_kernel,
        in_specs=[SMEM] + [VMEM] * 3,
        out_specs=VMEM,
        out_shape=sds((64, 40, 128), BF16),
        compiler_params=params(16),
        name="total",
    )(scal, received, gain_part, gain_far)
    gathered = lax.all_to_all(totals, "curve", 0, 0)

    grad_points = pl.pallas_call(
        place_kernel,
        grid_spec=pltpu.PrefetchScalarGridSpec(
            num_scalar_prefetch=1,
            grid=(slots,),
            in_specs=[
                pl.BlockSpec((slots, patch), lambda i, s: (0, 0)),
                SMEM,
                pl.BlockSpec((1, patch, 128), lambda i, s: (i, 0, s[1])),
                pl.BlockSpec((2, 128, patch), lambda i, s: (0, 0, 0)),
                pl.BlockSpec((128, half), lambda i, s: (0, 0)),
                pl.BlockSpec((128, half), lambda i, s: (0, 0)),
            ],
            out_specs=pl.BlockSpec((1, patch, 128), lambda i, s: (i, 0, 0)),
            scratch_shapes=[pltpu.VMEM((128, patch), BF16)],
        ),
        out_shape=sds((slots, patch, 128), BF16),
        compiler_params=params(16),
        cost_estimate=cost(10**10, 1000),
        name="place",
    )(scal, order, before, cotangent, branch, from_before, from_after)

    grad_qkv, grad_out, grad_gain = pl.pallas_call(
        finish_kernel,
        in_specs=[VMEM],
        out_specs=[VMEM] * 3,
        out_shape=[sds((3, width, 128), F32), sds((128, width), F32), sds((1, 128), F32)],
        compiler_params=params(16),
        name="finish",
    )(gathered)
    return grad_points, grad_gain.reshape(128), jnp.transpose(grad_qkv, (1, 0, 2)), grad_out


def solution(mesh):
    in_specs = (
        P("curve", None, None),
        P("curve", None),
        P("curve"),
        P("curve", None, None),
        P(),
        P(None, None, "mp"),
        P("mp", None),
    )
    out_specs = (P("curve", None, "mp"), P("mp"), P(None, None, "mp"), P("mp", None))
    return jax.shard_map(shards, mesh=mesh, in_specs=in_specs, out_specs=out_specs, check_vma=False)
```
